32 devices in a mesh: ens: 2 (over x), lon: 16 (over z, y, core).
Axes of the slice: x: 2, y: 2, z: 4, core: 2. Of those that a mesh axis runs over, the one named last changes fastest.
Arguments:
- state: float32 [192, 768, 256], P('ens', 'lon'), parts along dimension 0, may hold values from -6 to 6
- courant: float32 [192, 768, 128], P('ens', 'lon'), parts along dimension 0, may hold values from -0.45 to 0.45
- daylit: int32 [192, 768], P('ens', 'lon'), parts along dimension 0, may hold values from 0 to 1, as said below
- insolation: float32 [192, 768], P('ens', 'lon'), parts along dimension 0, may hold values from 0.1 to 1
- long_in: bfloat16 [256, 1024], replicated, may hold values from -0.375 to 0.375
- long_out: bfloat16 [1024, 256], replicated, may hold values from -0.1875 to 0.1875
- short_in: bfloat16 [256, 1024], replicated, may hold values from -0.375 to 0.375
- short_sun: bfloat16 [1024], replicated, may hold values from -4 to 4
- short_mid: bfloat16 [2, 1024, 1024], replicated, may hold values from -0.1875 to 0.1875
- short_out: bfloat16 [1024, 256], replicated, may hold values from -0.1875 to 0.1875
Outputs:
- new_state: float32 [192, 768, 256], P('ens', 'lon'), parts along dimension 0
- tendency: bfloat16 [192, 768, 256], P('ens', 'lon'), parts along dimension 0
The draws below stay inside these ranges and needn't reach their ends.
There are 2 independent parts, one for each index of `ens`. The reference program is written for one: setup_inputs(seed, part) draws one part's arguments, and reference() takes and returns one part's arrays. A program takes and returns all parts, laid end to end along the dimension named above; an argument that names none is the same for every part. Nothing has to cross between parts.
Inputs may be any that keep to these rules, and one draw needn't show every extreme that they name: In each latitude row the daylit columns are exactly 384 consecutive longitudes of the periodic circle, and the first of them lies within 48 longitudes of a point common to all rows of the part.
All inputs are finite; a program needn't handle non-finite values.
Results may differ from the reference program's by a relative error of at most 0.006.
Values may be sent and summed in bfloat16 or wider, within the bound.
No kernel may reach another device: no remote copies, remote signals or barrier semaphores. Data moves between devices by JAX's collectives and lax.ppermute only.
A program may use at most 128 MiB of HBM per device.

```python
import jax
import jax.numpy as jnp
from jax import lax

L = 128
HID = 1024
NLAT = 96
CLON = 48
NLON = 768


def draw_daylit(key, part):
    key = jax.random.fold_in(key, 7)
    start_key, jitter_key = jax.random.split(key)
    start = jax.random.randint(start_key, (), 0, NLON)
    jitter = jax.random.randint(jitter_key, (NLAT,), -CLON, CLON + 1)
    first = start + jitter
    longitude = jnp.arange(NLON)
    offset = (longitude[None, :] - first[:, None]) % NLON
    return (offset < NLON // 2).astype(jnp.int32)


def shard_levels(rng, extent, shards, low, largest):
    level, own = 1.0, jax.random.fold_in(rng, 6)
    for axis_at, parts in shards:
        steps = jnp.exp(jax.random.uniform(jax.random.fold_in(own, axis_at), (parts,), jnp.float32, low / len(shards), largest / len(shards)))
        level = level * jnp.repeat(steps, extent[axis_at] // parts).reshape([-1 if axis == axis_at else 1 for axis in range(len(extent))])
    return level


def noise(own_key, dims, deviation, limit, cuts=(), held_as=jnp.bfloat16):
    array = jax.random.normal(own_key, dims, jnp.float32) * deviation
    if len(cuts) > 0:
        array = shard_levels(own_key, dims, cuts, -0.22, 0.18) * array
    return jnp.clip(array, min=-limit, max=limit).astype(held_as)


def setup_inputs(seed: int = 0, part: int = 0) -> dict:
    key_of = jax.random.split(jax.random.key(seed), 11)
    part_keys = jax.random.split(jax.random.fold_in(key_of[10], part), 11)
    state = noise(part_keys[0], (NLAT, NLON, 2 * L), 1.0, 6.0, ((1, 16),), jnp.float32)
    courant = jnp.clip(jax.random.uniform(part_keys[1], (NLAT, NLON, L), jnp.float32, -0.45, 0.45) * shard_levels(part_keys[1], (NLAT, NLON, L), ((1, 16),), -0.4, 0.0), -0.45, 0.45)
    daylit = draw_daylit(jax.random.fold_in(jax.random.fold_in(key_of[10], part), 71), part)
    insolation = jnp.clip(0.1 + 0.9 * jax.random.uniform(part_keys[3], (NLAT, NLON), jnp.float32) ** shard_levels(part_keys[3], (NLAT, NLON), ((1, 16),), -0.2, 0.2), 0.1, 1.0)
    long_in = noise(key_of[4], (2 * L, HID), (2 * L) ** -0.5, 0.375)
    long_out = noise(key_of[5], (HID, 2 * L), HID ** -0.5, 0.1875)
    short_in = noise(key_of[6], (2 * L, HID), (2 * L) ** -0.5, 0.375)
    short_sun = noise(key_of[7], (HID,), 1.0, 4.0)
    short_mid = noise(key_of[8], (2, HID, HID), HID ** -0.5, 0.1875)
    short_out = noise(key_of[9], (HID, 2 * L), HID ** -0.5, 0.1875)
    return dict(state=state, courant=courant, daylit=daylit, insolation=insolation, long_in=long_in, long_out=long_out, short_in=short_in, short_sun=short_sun, short_mid=short_mid, short_out=short_out)


def long_net(columns, long_in, long_out):
    hidden = jax.nn.silu(jnp.dot(columns, long_in, preferred_element_type=jnp.float32)).astype(jnp.bfloat16)
    return jnp.dot(hidden, long_out, preferred_element_type=jnp.float32)


def short_net(columns, sunlight, short_in, short_sun, short_mid, short_out):
    first = jnp.dot(columns, short_in, preferred_element_type=jnp.float32)
    first = first + sunlight[:, None] * short_sun.astype(jnp.float32)[None, :]
    hidden = jax.nn.silu(first).astype(jnp.bfloat16)
    hidden = jax.nn.silu(jnp.dot(hidden, short_mid[0], preferred_element_type=jnp.float32)).astype(jnp.bfloat16)
    hidden = jax.nn.silu(jnp.dot(hidden, short_mid[1], preferred_element_type=jnp.float32)).astype(jnp.bfloat16)
    return jnp.dot(hidden, short_out, preferred_element_type=jnp.float32).astype(jnp.bfloat16)


def reference(state, courant, daylit, insolation, long_in, long_out, short_in, short_sun, short_mid, short_out):
    features = 2 * L
    columns = state.astype(jnp.bfloat16)
    long_tend = lax.map(lambda row_cols: long_net(row_cols, long_in, long_out), columns)
    flat_cols = columns.reshape(NLAT * NLON, features)
    flat_mask = daylit.reshape(NLAT * NLON)
    flat_sun = insolation.reshape(NLAT * NLON)
    lit_count = NLAT * NLON // 2
    lit_index = jnp.nonzero(flat_mask, size=lit_count)[0].astype(jnp.int32)
    picked = flat_cols[lit_index].reshape(NLAT, NLON // 2, features)
    picked_sun = flat_sun[lit_index].reshape(NLAT, NLON // 2)
    short_vals = lax.map(lambda pair: short_net(pair[0], pair[1], short_in, short_sun, short_mid, short_out), (picked, picked_sun))
    short_flat = jnp.zeros((NLAT * NLON, features), jnp.bfloat16).at[lit_index].set(short_vals.reshape(lit_count, features))
    short_tend = short_flat.reshape(NLAT, NLON, features)
    physics = long_tend + daylit[:, :, None].astype(jnp.float32) * short_tend.astype(jnp.float32)
    tendency = physics.astype(jnp.bfloat16)
    provisional = state + physics
    courant_pair = jnp.concatenate([courant, courant], axis=-1)
    east_flux = jnp.maximum(courant_pair, 0.0) * provisional + jnp.minimum(courant_pair, 0.0) * jnp.roll(provisional, -1, axis=1)
    new_state = provisional - (east_flux - jnp.roll(east_flux, 1, axis=1))
    return new_state, tendency
```

```python
import functools

import jax
import jax.numpy as jnp
from jax import lax
from jax.experimental import pallas as pl
from jax.experimental.pallas import tpu as pltpu
from jax.sharding import PartitionSpec as P

BF16 = jnp.bfloat16
F32 = jnp.float32


def dot(a, b):
    return jnp.dot(a, b, preferred_element_type=F32)


def silu_of_twice(h):
    return (h + h * jnp.tanh(h)).astype(BF16)


def nets(half_cols, sun_col, w, first_step):
    long_in, long_out, short_in, short_sun, short_mid, short_out, ready = w
    half_sun = sun_col * 0.5
    sun_row = short_sun[...].astype(F32)
    ready(0, first_step)
    first = silu_of_twice(dot(half_cols, short_in[...]) + half_sun * sun_row)
    ready(1, first_step)
    hidden = silu_of_twice(dot(half_cols, long_in[...]))
    ready(2, first_step)
    second = silu_of_twice(dot(first, short_mid[0]) * 0.5)
    ready(3, first_step)
    long_tend = dot(hidden, long_out[...])
    ready(4, first_step)
    third = silu_of_twice(dot(second, short_mid[1]) * 0.5)
    ready(5, first_step)
    short_tend = dot(third, short_out[...])
    return long_tend + jnp.where(sun_col > 0.0, short_tend, 0.0)


def weight_copies(hbm, vmem, sems):
    long_in, long_out, short_in, short_mid, short_out = hbm
    v_long_in, v_long_out, v_short_in, v_short_mid, v_short_out = vmem
    pairs = (
        (short_in, v_short_in),
        (long_in, v_long_in),
        (short_mid.at[0], v_short_mid.at[0]),
        (long_out, v_long_out),
        (short_mid.at[1], v_short_mid.at[1]),
        (short_out, v_short_out),
    )
    return [pltpu.make_async_copy(s, d, sems.at[k]) for k, (s, d) in enumerate(pairs)]


def staged_weights(hbm, vmem, sems, short_sun, first_step):
    copies = weight_copies(hbm, vmem, sems)

    @pl.when(first_step)
    def _():
        for copy in copies:
            copy.start()

    def ready(k, at_first):
        @pl.when(at_first)
        def _():
            copies[k].wait()

    long_in, long_out, short_in, short_mid, short_out = vmem
    return (long_in, long_out, short_in, short_sun, short_mid, short_out, ready)


def lit_sun_column(day_ref, sun_ref, row0, rows):
    lit = jnp.where(day_ref[...] > 0, sun_ref[...], 0.0)
    lane = lax.broadcasted_iota(jnp.int32, lit.shape, 1)
    return jnp.concatenate(
        [
            jnp.sum(jnp.where(lane == row0 + r, lit, 0.0), axis=1, keepdims=True)
            for r in range(rows)
        ],
        axis=0,
    )


def first_kernel(
    rows, day, sun, state, long_in, long_out, short_in, short_sun, short_mid, short_out,
    tend, v0, v1, v2, v3, v4, sems,
):
    i = pl.program_id(0)
    first_step = i == 0
    w = staged_weights(
        (long_in, long_out, short_in, short_mid, short_out), (v0, v1, v2, v3, v4), sems, short_sun, first_step
    )
    _, cells, feats = state.shape[1:]
    cols = rows * cells
    sun_col = lit_sun_column(day, sun, i * rows, rows)
    half_cols = (state[0].reshape(cols, feats) * 0.5).astype(BF16)
    phys = nets(half_cols, sun_col, w, first_step)
    tend[0] = phys.astype(BF16).reshape(rows, cells, feats)


def transport(prov, courant, west_prov, west_cour, east_prov):
    rows, cells, feats = prov.shape
    cols = rows * cells
    pair = jnp.concatenate([courant, courant], axis=-1)
    east_wind, west_wind = jnp.maximum(pair, 0.0), jnp.minimum(pair, 0.0)
    sub = lax.broadcasted_iota(jnp.int32, (rows, 8, feats), 1)
    nxt = pltpu.roll(prov.reshape(cols, feats), cols - 1, 0).reshape(rows, cells, feats)
    tail = jnp.where(sub == 7, east_prov[:, None, :], nxt[:, cells - 8 :])
    nxt = jnp.concatenate([nxt[:, : cells - 8], tail], axis=1)
    flux = east_wind * prov + west_wind * nxt
    prev = pltpu.roll(flux.reshape(cols, feats), 1, 0).reshape(rows, cells, feats)
    wc = jnp.concatenate([west_cour, west_cour], axis=-1)
    face = (jnp.maximum(wc, 0.0) * west_prov)[:, None, :] + jnp.minimum(wc, 0.0)[:, None, :] * prov[:, :8]
    head = jnp.where(sub == 0, face, prev[:, :8])
    prev = jnp.concatenate([head, prev[:, 8:]], axis=1)
    return prov - (flux - prev)


def second_kernel(
    rows, day, sun, state, courant, west_a, west_b, east_a, east_b, tend_in,
    long_in, long_out, short_in, short_sun, short_mid, short_out,
    new_state, tend, v0, v1, v2, v3, v4, sems,
):
    i = pl.program_id(0)
    first_step = i == 0
    w = staged_weights(
        (long_in, long_out, short_in, short_mid, short_out), (v0, v1, v2, v3, v4), sems, short_sun, first_step
    )
    _, cells, feats = state.shape[1:]
    cols = rows * cells
    levels = courant.shape[-1]
    sun_col = lit_sun_column(day, sun, (pl.num_programs(0) + i) * rows, rows)
    halos = (west_a, west_b, east_a, east_b)
    sun_all = jnp.concatenate([sun_col] + [h[:, -1:].astype(F32) for h in halos], axis=0)
    half_cols = jnp.concatenate(
        [(state[1].reshape(cols, feats) * 0.5).astype(BF16)] + [h[:, :feats] * 0.5 for h in halos], axis=0
    )
    phys = nets(half_cols, sun_all, w, first_step)
    own = phys[:cols].reshape(rows, cells, feats)
    tend[0] = own.astype(BF16)
    edge = [
        h[:, :feats].astype(F32) + phys[cols + k * rows : cols + (k + 1) * rows] for k, h in enumerate(halos)
    ]
    new_state[0] = transport(
        state[0] + tend_in[0].astype(F32), courant[0],
        edge[0], west_a[:, feats : feats + levels].astype(F32), edge[2],
    )
    new_state[1] = transport(
        state[1] + own, courant[1],
        edge[1], west_b[:, feats : feats + levels].astype(F32), edge[3],
    )


def shards(
    state, courant, daylit, insolation, long_in, long_out, short_in, short_sun, short_mid, short_out
):
    lat_rows, cells, feats = state.shape
    levels = courant.shape[-1]
    hid = long_in.shape[1]
    size = lax.axis_size("lon")
    up = [(i, (i + 1) % size) for i in range(size)]
    down = [(j, i) for i, j in up]

    def packed(at, with_courant):
        lit = jnp.where(daylit[:, at] > 0, insolation[:, at], 0.0)
        parts = [state[:, at]] + ([courant[:, at]] if with_courant else [])
        parts.append(jnp.broadcast_to(lit[:, None], (lat_rows, 128)))
        return jnp.concatenate(parts, axis=-1).astype(BF16)

    west = lax.ppermute(packed(cells - 1, True), "lon", up)
    east = lax.ppermute(packed(0, False), "lon", down)

    half = lat_rows // 2
    rows = 16
    steps = half // rows
    day_t, sun_t = daylit.T, insolation.T
    state4 = state.reshape(2, half, cells, feats)
    courant4 = courant.reshape(2, half, cells, levels)
    sun_row = short_sun.reshape(1, hid)
    weights = (long_in, long_out, short_in, sun_row, short_mid, short_out)
    any_spec = pl.BlockSpec(memory_space=pl.ANY)
    small = pl.BlockSpec((cells, lat_rows), lambda i: (0, 0))
    weight_specs = [any_spec, any_spec, any_spec, pl.BlockSpec((1, hid), lambda i: (0, 0)), any_spec, any_spec]
    scratch = [
        pltpu.VMEM((feats, hid), BF16),
        pltpu.VMEM((hid, feats), BF16),
        pltpu.VMEM((feats, hid), BF16),
        pltpu.VMEM((2, hid, hid), BF16),
        pltpu.VMEM((hid, feats), BF16),
        pltpu.SemaphoreType.DMA((6,)),
    ]
    macs = 4 * feats * hid + 2 * hid * hid

    def grid_block(lead, last, at):
        return pl.BlockSpec((lead, rows, cells, last), lambda i: (at, i, 0, 0))

    params = pltpu.CompilerParams(vmem_limit_bytes=48 * 2**20)
    tend_shape = jax.ShapeDtypeStruct((2, half, cells, feats), BF16)
    tend = pl.pallas_call(
        functools.partial(first_kernel, rows),
        grid=(steps,),
        in_specs=[small, small, grid_block(1, feats, 0)] + weight_specs,
        out_specs=grid_block(1, feats, 0),
        out_shape=tend_shape,
        scratch_shapes=scratch,
        compiler_params=params,
        cost_estimate=pl.CostEstimate(
            flops=2 * half * cells * macs, bytes_accessed=10 * 2**20, transcendentals=0
        ),
        name="nets_first_half",
    )(day_t, sun_t, state4, *weights)

    def halo_spec(last, offset):
        return pl.BlockSpec((rows, last), lambda i: (i + offset, 0))

    new_state, tend = pl.pallas_call(
        functools.partial(second_kernel, rows),
        grid=(steps,),
        in_specs=[
            small, small, grid_block(2, feats, 0), grid_block(2, levels, 0),
            halo_spec(feats + levels + 128, 0), halo_spec(feats + levels + 128, steps),
            halo_spec(feats + 128, 0), halo_spec(feats + 128, steps),
            grid_block(1, feats, 0),
        ] + weight_specs,
        out_specs=(grid_block(2, feats, 0), grid_block(1, feats, 1)),
        out_shape=(jax.ShapeDtypeStruct((2, half, cells, feats), F32), tend_shape),
        input_output_aliases={8: 1},
        scratch_shapes=scratch,
        compiler_params=params,
        cost_estimate=pl.CostEstimate(
            flops=2 * half * (cells + 4) * macs, bytes_accessed=24 * 2**20, transcendentals=0
        ),
        name="nets_second_half_transport",
    )(day_t, sun_t, state4, courant4, west, west, east, east, tend, *weights)
    return new_state.reshape(state.shape), tend.reshape(state.shape)


def solution(mesh):
    in_specs = (
        P("ens", "lon", None),
        P("ens", "lon", None),
        P("ens", "lon"),
        P("ens", "lon"),
        P(),
        P(),
        P(),
        P(),
        P(),
        P(),
    )
    out_specs = (P("ens", "lon", None), P("ens", "lon", None))
    return jax.shard_map(shards, mesh=mesh, in_specs=in_specs, out_specs=out_specs, check_vma=False)
```

```python
import functools

import jax
import jax.numpy as jnp
from jax import lax
from jax.experimental import pallas as pl
from jax.experimental.pallas import tpu as pltpu
from jax.sharding import PartitionSpec as P

BF16 = jnp.bfloat16
F32 = jnp.float32


def dot(a, b):
    return jnp.dot(a, b, preferred_element_type=F32)


def silu_of_twice(h):
    return (h + h * jnp.tanh(h)).astype(BF16)


def nets(half_cols, sun_col, w):
    long_in, long_out, short_in, short_sun, short_mid, short_out = w
    half_sun = sun_col * 0.5
    sun_row = short_sun[...].astype(F32)
    first = silu_of_twice(dot(half_cols, short_in[...]) + half_sun * sun_row)
    hidden = silu_of_twice(dot(half_cols, long_in[...]))
    second = silu_of_twice(dot(first, short_mid[0]) * 0.5)
    long_tend = dot(hidden, long_out[...])
    third = silu_of_twice(dot(second, short_mid[1]) * 0.5)
    short_tend = dot(third, short_out[...])
    return long_tend + jnp.where(sun_col > 0.0, short_tend, 0.0)


def lit_sun_column(day_ref, sun_ref, row0, rows):
    lit = jnp.where(day_ref[...] > 0, sun_ref[...], 0.0)
    lane = lax.broadcasted_iota(jnp.int32, lit.shape, 1)
    return jnp.concatenate(
        [
            jnp.sum(jnp.where(lane == row0 + r, lit, 0.0), axis=1, keepdims=True)
            for r in range(rows)
        ],
        axis=0,
    )


def pack_kernel(day, sun, state_w, state_e, courant_w, courant_e, out_a, out_b):
    feats, levels = state_w.shape[-1], courant_w.shape[-1]
    end = feats + levels
    cells, lat_rows = day.shape
    odd = lax.rem(lax.axis_index("lon"), 2) == 1
    lit = jnp.where(day[...] > 0, sun[...], 0.0)

    def choose(east, west):
        return jnp.where(odd, west, east).astype(BF16), jnp.where(odd, east, west).astype(BF16)

    for lanes, (a, b) in (
        (slice(0, feats), choose(state_e[:, 7, :], state_w[:, 0, :])),
        (slice(feats, end), choose(courant_e[:, 7, :], courant_w[:, 0, :])),
    ):
        out_a[:, lanes] = a
        out_b[:, lanes] = b
    for out, row in zip((out_a, out_b), choose(lit[cells - 1 :], lit[:1])):
        out[:, end:] = jnp.zeros((lat_rows, out.shape[1] - end), BF16)
        out[:16, end : end + lat_rows] = jnp.broadcast_to(row, (16, lat_rows))


def first_kernel(rows, day, sun, state, *rest):
    *w, tend = rest
    i = pl.program_id(0)
    _, _, cells, feats = state.shape
    cols = rows * cells
    sun_col = lit_sun_column(day, sun, i * rows, rows)
    half_cols = (state[0].reshape(cols, feats) * 0.5).astype(BF16)
    tend[0] = nets(half_cols, sun_col, w).astype(BF16).reshape(rows, cells, feats)


def transport(prov, courant, west_prov, west_cour, east_prov):
    rows, cells, feats = prov.shape
    cols = rows * cells
    pair = jnp.concatenate([courant, courant], axis=-1)
    east_wind, west_wind = jnp.maximum(pair, 0.0), jnp.minimum(pair, 0.0)
    sub = lax.broadcasted_iota(jnp.int32, (rows, 8, feats), 1)
    nxt = pltpu.roll(prov.reshape(cols, feats), cols - 1, 0).reshape(rows, cells, feats)
    tail = jnp.where(sub == 7, east_prov[:, None, :], nxt[:, cells - 8 :])
    nxt = jnp.concatenate([nxt[:, : cells - 8], tail], axis=1)
    flux = east_wind * prov + west_wind * nxt
    prev = pltpu.roll(flux.reshape(cols, feats), 1, 0).reshape(rows, cells, feats)
    wc = jnp.concatenate([west_cour, west_cour], axis=-1)
    face = (jnp.maximum(wc, 0.0) * west_prov)[:, None, :] + jnp.minimum(wc, 0.0)[:, None, :] * prov[:, :8]
    head = jnp.where(sub == 0, face, prev[:, :8])
    prev = jnp.concatenate([head, prev[:, 8:]], axis=1)
    return prov - (flux - prev)


def second_kernel(
    rows, day, sun, state, state_lo, courant, a_lo, a_hi, a_sun, b_lo, b_hi, b_sun, tend_lo,
    long_in, long_out, short_in, short_sun, short_mid, short_out,
    new_state, tend, prov, edges, west_wind,
):
    i = pl.program_id(0)
    tiles = pl.num_programs(0) - 1
    _, _, cells, feats = state.shape
    cols = rows * cells
    levels = courant.shape[-1]
    odd = lax.rem(lax.axis_index("lon"), 2) == 1

    def column_nets():
        row0 = (tiles + i) * rows
        sun_col = lit_sun_column(day, sun, row0, rows)
        west_lo = jnp.where(odd, a_lo[0].astype(F32), b_lo[0].astype(F32))
        west_hi = jnp.where(odd, a_hi[0].astype(F32), b_hi[0].astype(F32))
        east_lo = jnp.where(odd, b_lo[1].astype(F32), a_lo[1].astype(F32))
        east_hi = jnp.where(odd, b_hi[1].astype(F32), a_hi[1].astype(F32))
        halos = [h[:, :feats] for h in (west_lo, west_hi, east_lo, east_hi)]
        lat_rows = day.shape[1]
        west_sun = jnp.where(odd, a_sun[0].astype(F32), b_sun[0].astype(F32))
        east_sun = jnp.where(odd, b_sun[1].astype(F32), a_sun[1].astype(F32))
        lane = lax.broadcasted_iota(jnp.int32, west_sun.shape, 1)
        sub = lax.broadcasted_iota(jnp.int32, west_sun.shape, 0)
        suns = [
            jnp.sum(jnp.where(lane == sub + at, lit, 0.0), axis=1, keepdims=True)
            for lit, at in ((west_sun, i * rows), (west_sun, row0), (east_sun, i * rows), (east_sun, row0))
        ]
        sun_all = jnp.concatenate([sun_col] + suns, axis=0)
        own_state = state[0].reshape(cols, feats)
        half_cols = (jnp.concatenate([own_state] + halos, axis=0) * 0.5).astype(BF16)
        phys = nets(half_cols, sun_all, (long_in, long_out, short_in, short_sun, short_mid, short_out))
        tend[0] = phys[:cols].astype(BF16).reshape(rows, cells, feats)
        prov[...] = (own_state + phys[:cols]).reshape(rows, cells, feats)
        edges[...] = jnp.concatenate(halos, axis=0) + phys[cols:]
        west_wind[...] = jnp.concatenate([west_lo, west_hi], axis=0)[:, feats : feats + levels]

    def move():
        new_state[0] = transport(
            state_lo[0] + tend_lo[0].astype(F32), courant[0],
            edges[:rows], west_wind[:rows], edges[2 * rows : 3 * rows],
        )
        new_state[1] = transport(
            prov[...], courant[1], edges[rows : 2 * rows], west_wind[rows:], edges[3 * rows :],
        )

    @pl.when(i == 0)
    def _():
        column_nets()

    @pl.when(jnp.logical_and(i > 0, i < tiles))
    def _():
        move()
        column_nets()

    @pl.when(i == tiles)
    def _():
        move()


def exchange(edge_a, edge_b, pairs, seams):
    return (
        lax.all_gather(edge_a, "lon", axis_index_groups=pairs),
        lax.all_gather(edge_b, "lon", axis_index_groups=seams),
    )


def shards(
    state, courant, daylit, insolation, long_in, long_out, short_in, short_sun, short_mid, short_out
):
    lat_rows, cells, feats = state.shape
    levels = courant.shape[-1]
    hid = long_in.shape[1]
    size = lax.axis_size("lon")
    rows = 16
    half = lat_rows // 2
    steps = half // rows
    width = feats + levels + 128
    day_t, sun_t = daylit.T, insolation.T
    small = pl.BlockSpec((cells, lat_rows), lambda *i: (0, 0))
    last = cells // 8 - 1

    def edge_block(depth, at):
        return pl.BlockSpec((lat_rows, 8, depth), lambda i: (0, at, 0))

    edge_shape = jax.ShapeDtypeStruct((lat_rows, width), BF16)
    edge_out = pl.BlockSpec((lat_rows, width), lambda i: (0, 0))
    edge_a, edge_b = pl.pallas_call(
        pack_kernel,
        grid=(1,),
        in_specs=[small, small, edge_block(feats, 0), edge_block(feats, last), edge_block(levels, 0), edge_block(levels, last)],
        out_specs=(edge_out, edge_out),
        out_shape=(edge_shape, edge_shape),
        cost_estimate=pl.CostEstimate(flops=0, bytes_accessed=3 * 2**20, transcendentals=0),
        name="edges_packed",
    )(day_t, sun_t, state, state, courant, courant)
    pairs = [[i, i + 1] for i in range(0, size, 2)]
    seams = [[i, (i + 1) % size] for i in range(1, size, 2)]
    halo_a, halo_b = exchange(edge_a, edge_b, pairs, seams)

    state4 = state.reshape(2, half, cells, feats)
    courant4 = courant.reshape(2, half, cells, levels)
    weights = tuple(
        pltpu.with_memory_space_constraint(w, pltpu.VMEM)
        for w in (long_in, long_out, short_in, short_sun.reshape(1, hid), short_mid, short_out)
    )
    weight_specs = [pl.BlockSpec(memory_space=pltpu.VMEM)] * 6
    macs = 4 * feats * hid + 2 * hid * hid
    params = pltpu.CompilerParams(vmem_limit_bytes=44 * 2**20)
    tend_shape = jax.ShapeDtypeStruct((2, half, cells, feats), BF16)
    tend = pl.pallas_call(
        functools.partial(first_kernel, rows),
        grid=(steps,),
        in_specs=[small, small, pl.BlockSpec((1, rows, cells, feats), lambda i: (0, i, 0, 0))] + weight_specs,
        out_specs=pl.BlockSpec((1, rows, cells, feats), lambda i: (0, i, 0, 0)),
        out_shape=tend_shape,
        compiler_params=params,
        cost_estimate=pl.CostEstimate(
            flops=2 * half * cells * macs, bytes_accessed=10 * 2**20, transcendentals=0
        ),
        name="nets_first_half",
    )(day_t, sun_t, state4, *weights)

    def here(i):
        return jnp.minimum(i, steps - 1)

    def before(i):
        return jnp.maximum(i - 1, 0)

    def block(lead, depth, at, when):
        return pl.BlockSpec((lead, rows, cells, depth), lambda i: (at, when(i), 0, 0))

    halo_lo = pl.BlockSpec((2, rows, width), lambda i: (0, here(i), 0))
    halo_hi = pl.BlockSpec((2, rows, width), lambda i: (0, steps + here(i), 0))
    halo_sun = pl.BlockSpec((2, 16, 128), lambda i: (0, 0, width // 128 - 1))
    new_state, tend = pl.pallas_call(
        functools.partial(second_kernel, rows),
        grid=(steps + 1,),
        in_specs=[
            small, small, block(1, feats, 1, here), block(1, feats, 0, before), block(2, levels, 0, before),
            halo_lo, halo_hi, halo_sun, halo_lo, halo_hi, halo_sun,
            block(1, feats, 0, before),
        ] + weight_specs,
        out_specs=(block(2, feats, 0, before), block(1, feats, 1, here)),
        out_shape=(jax.ShapeDtypeStruct((2, half, cells, feats), F32), tend_shape),
        input_output_aliases={11: 1},
        scratch_shapes=[
            pltpu.VMEM((rows, cells, feats), F32),
            pltpu.VMEM((4 * rows, feats), F32),
            pltpu.VMEM((2 * rows, levels), F32),
        ],
        compiler_params=params,
        cost_estimate=pl.CostEstimate(
            flops=2 * half * (cells + 4) * macs, bytes_accessed=24 * 2**20, transcendentals=0
        ),
        name="nets_second_half_transport",
    )(day_t, sun_t, state4, state4, courant4, halo_a, halo_a, halo_a, halo_b, halo_b, halo_b, tend, *weights)
    return new_state.reshape(state.shape), tend.reshape(state.shape)


def solution(mesh):
    in_specs = (
        P("ens", "lon", None),
        P("ens", "lon", None),
        P("ens", "lon"),
        P("ens", "lon"),
        P(),
        P(),
        P(),
        P(),
        P(),
        P(),
    )
    out_specs = (P("ens", "lon", None), P("ens", "lon", None))
    return jax.shard_map(shards, mesh=mesh, in_specs=in_specs, out_specs=out_specs, check_vma=False)
```

```python
import functools

import jax
import jax.numpy as jnp
from jax import lax
from jax.experimental import pallas as pl
from jax.experimental.pallas import tpu as pltpu
from jax.sharding import PartitionSpec as P

BF16 = jnp.bfloat16
F32 = jnp.float32


def dot(a, b):
    return jnp.dot(a, b, preferred_element_type=F32)


def silu_of_twice(h):
    return (h + h * jnp.tanh(h)).astype(BF16)


def nets(half_cols, sun_col, w):
    long_in, long_out, short_in, short_sun, short_mid, short_out = w
    half_sun = sun_col * 0.5
    sun_row = short_sun[...]
    first = silu_of_twice(dot(half_cols, short_in[...]) + half_sun * sun_row)
    hidden = silu_of_twice(dot(half_cols, long_in[...]))
    second = silu_of_twice(dot(first, short_mid[0]) * 0.5)
    long_tend = dot(hidden, long_out[...])
    third = silu_of_twice(dot(second, short_mid[1]) * 0.5)
    short_tend = dot(third, short_out[...])
    return long_tend + jnp.where(sun_col > 0.0, short_tend, 0.0)


def lit_sun_column(day_ref, sun_ref, row0, rows):
    lit = jnp.where(day_ref[...] > 0, sun_ref[...], 0.0)
    lane = lax.broadcasted_iota(jnp.int32, lit.shape, 1)
    return jnp.concatenate(
        [
            jnp.sum(jnp.where(lane == row0 + r, lit, 0.0), axis=1, keepdims=True)
            for r in range(rows)
        ],
        axis=0,
    )


def pack_kernel(
    day_hbm, sun_hbm, short_sun_hbm, state, courant, out_a, out_b, sun_row,
    day, sun, short_sun, west, east, wind, sems,
):
    feats, levels = state.shape[-1], courant.shape[-1]
    end = feats + levels
    cells, lat_rows = day.shape
    copies = [
        pltpu.make_async_copy(src, dst, sems.at[k])
        for k, (src, dst) in enumerate((
            (state.at[:, pl.ds(0, 8), :], west),
            (state.at[:, pl.ds(cells - 8, 8), :], east),
            (courant.at[:, pl.ds(cells - 8, 8), :], wind),
            (day_hbm, day),
            (sun_hbm, sun),
            (short_sun_hbm, short_sun),
        ))
    ]
    for copy in copies:
        copy.start()
    for copy in copies[3:]:
        copy.wait()
    odd = lax.rem(lax.axis_index("lon"), 2) == 1
    lit = jnp.where(day[...] > 0, sun[...], 0.0)

    def choose(to_east, to_west):
        a, b = jnp.where(odd, to_west, to_east), jnp.where(odd, to_east, to_west)
        return a.astype(BF16), b.astype(BF16)

    sun_row[...] = short_sun[...].astype(F32).reshape(sun_row.shape)
    for out, row in zip((out_a, out_b), choose(lit[cells - 1 :], lit[:1])):
        out[:, end:] = jnp.zeros((lat_rows, out.shape[1] - end), BF16)
        out[:16, end : end + lat_rows] = jnp.broadcast_to(row, (16, lat_rows))
    for copy in copies[:3]:
        copy.wait()
    out_a[:, :feats], out_b[:, :feats] = choose(east[:, 7, :], west[:, 0, :])
    out_a[:, feats:end] = wind[:, 7, :].astype(BF16)
    out_b[:, feats:end] = wind[:, 7, :].astype(BF16)


def first_kernel(rows, day, sun, state, *rest):
    *w, tend, prov = rest
    row0 = pl.multiple_of(pl.program_id(0) * rows, rows)
    _, cells, feats = state.shape
    cols = rows * cells
    sun_col = lit_sun_column(day, sun, row0, rows)
    own = state[pl.ds(row0, rows)].reshape(cols, feats)
    phys = nets((own * 0.5).astype(BF16), sun_col, w)
    tend[0] = phys.astype(BF16).reshape(rows, cells, feats)
    prov[pl.ds(row0, rows)] = (own + phys).reshape(rows, cells, feats)


def transport(prov, courant, west_prov, west_cour, east_prov):
    rows, cells, feats = prov.shape
    cols = rows * cells
    pair = jnp.concatenate([courant, courant], axis=-1)
    east_wind, west_wind = jnp.maximum(pair, 0.0), jnp.minimum(pair, 0.0)
    sub = lax.broadcasted_iota(jnp.int32, (rows, 8, feats), 1)
    nxt = pltpu.roll(prov.reshape(cols, feats), cols - 1, 0).reshape(rows, cells, feats)
    tail = jnp.where(sub == 7, east_prov[:, None, :], nxt[:, cells - 8 :])
    nxt = jnp.concatenate([nxt[:, : cells - 8], tail], axis=1)
    flux = east_wind * prov + west_wind * nxt
    prev = pltpu.roll(flux.reshape(cols, feats), 1, 0).reshape(rows, cells, feats)
    wc = jnp.concatenate([west_cour, west_cour], axis=-1)
    face = (jnp.maximum(wc, 0.0) * west_prov)[:, None, :] + jnp.minimum(wc, 0.0)[:, None, :] * prov[:, :8]
    head = jnp.where(sub == 0, face, prev[:, :8])
    prev = jnp.concatenate([head, prev[:, 8:]], axis=1)
    return prov - (flux - prev)


def second_kernel(
    rows, day, sun, state, courant, halo_a, halo_b, prov_lo, tend_in,
    long_in, long_out, short_in, short_sun, short_mid, short_out,
    new_state, tend, prov, edges, west_wind,
):
    i = pl.program_id(0)
    tiles = pl.num_programs(0) - 1
    half = tiles * rows
    _, cells, feats = state.shape
    cols = rows * cells
    levels = courant.shape[-1]
    end = feats + levels
    lat_rows = day.shape[1]
    odd = lax.rem(lax.axis_index("lon"), 2) == 1

    def column_nets():
        lo = pl.multiple_of(i * rows, rows)
        hi = pl.multiple_of(half + i * rows, rows)

        def sides(at, n, lanes):
            a, b = halo_a[pl.ds(at, n), lanes].astype(F32), halo_b[pl.ds(at, n), lanes].astype(F32)
            return jnp.where(odd, a, b), jnp.where(odd, b, a)

        west_lo, east_lo = sides(lo, rows, slice(0, feats))
        west_hi, east_hi = sides(hi, rows, slice(0, feats))
        halos = [west_lo, west_hi, east_lo, east_hi]
        west_sun, east_sun = sides(0, 16, slice(end, end + 128))
        lane = lax.broadcasted_iota(jnp.int32, (rows, 128), 1)
        sub = lax.broadcasted_iota(jnp.int32, (rows, 128), 0)
        suns = [
            jnp.sum(jnp.where(lane == sub + at, lit, 0.0), axis=1, keepdims=True)
            for lit, at in ((west_sun, lo), (west_sun, hi), (east_sun, lo), (east_sun, hi))
        ]
        sun_all = jnp.concatenate([lit_sun_column(day, sun, hi, rows)] + suns, axis=0)
        own = state[pl.ds(hi, rows)].reshape(cols, feats)
        half_cols = (jnp.concatenate([own] + halos, axis=0) * 0.5).astype(BF16)
        phys = nets(half_cols, sun_all, (long_in, long_out, short_in, short_sun, short_mid, short_out))
        tend[0] = phys[:cols].astype(BF16).reshape(rows, cells, feats)
        prov[...] = (own + phys[:cols]).reshape(rows, cells, feats)
        edges[...] = jnp.concatenate(halos, axis=0) + phys[cols:]
        west_wind[:rows] = sides(lo, rows, slice(feats, end))[0]
        west_wind[rows:] = sides(hi, rows, slice(feats, end))[0]

    def move():
        lo = pl.multiple_of((i - 1) * rows, rows)
        new_state[0] = transport(
            prov_lo[pl.ds(lo, rows)], courant[pl.ds(lo, rows)],
            edges[:rows], west_wind[:rows], edges[2 * rows : 3 * rows],
        )
        new_state[1] = transport(
            prov[...], courant[pl.ds(half + lo, rows)],
            edges[rows : 2 * rows], west_wind[rows:], edges[3 * rows :],
        )

    @pl.when(i == 0)
    def _():
        column_nets()

    @pl.when(jnp.logical_and(i > 0, i < tiles))
    def _():
        move()
        column_nets()

    @pl.when(i == tiles)
    def _():
        move()


def shards(
    state, courant, daylit, insolation, long_in, long_out, short_in, short_sun, short_mid, short_out
):
    lat_rows, cells, feats = state.shape
    levels = courant.shape[-1]
    hid = long_in.shape[1]
    size = lax.axis_size("lon")
    rows = 16
    half = lat_rows // 2
    steps = half // rows
    width = feats + levels + 128
    day_t, sun_t = daylit.T, insolation.T
    in_vmem = pl.BlockSpec(memory_space=pltpu.VMEM)
    in_hbm = pl.BlockSpec(memory_space=pltpu.HBM)
    edge = pltpu.VMEM((lat_rows, width), BF16)
    edge_a, edge_b, sun_row = pl.pallas_call(
        pack_kernel,
        in_specs=[in_hbm] * 5,
        out_specs=(in_vmem,) * 3,
        out_shape=(edge, edge, pltpu.VMEM((1, hid), F32)),
        scratch_shapes=[
            pltpu.VMEM((cells, lat_rows), jnp.int32),
            pltpu.VMEM((cells, lat_rows), F32),
            pltpu.VMEM((hid,), BF16),
            pltpu.VMEM((lat_rows, 8, feats), F32),
            pltpu.VMEM((lat_rows, 8, feats), F32),
            pltpu.VMEM((lat_rows, 8, levels), F32),
            pltpu.SemaphoreType.DMA((6,)),
        ],
        compiler_params=pltpu.CompilerParams(vmem_limit_bytes=8 * 2**20),
        cost_estimate=pl.CostEstimate(flops=0, bytes_accessed=8 * 2**20, transcendentals=0),
        name="edges_packed",
    )(*(pltpu.with_memory_space_constraint(x, pltpu.HBM) for x in (day_t, sun_t, short_sun, state, courant)))
    flip = [(i, i ^ 1) for i in range(size)]
    seam = [(i, (i + 1 if i % 2 else i - 1) % size) for i in range(size)]
    halo_a = lax.ppermute(edge_a, "lon", flip)
    halo_b = lax.ppermute(edge_b, "lon", seam)

    def vmem(x):
        return pltpu.with_memory_space_constraint(x, pltpu.VMEM)

    weights = (vmem(long_in), vmem(long_out), vmem(short_in), sun_row, vmem(short_mid), vmem(short_out))
    macs = 4 * feats * hid + 2 * hid * hid
    params = pltpu.CompilerParams(vmem_limit_bytes=30 * 2**20)
    tend_shape = pltpu.HBM((2, half, cells, feats), BF16)
    v_state, v_day, v_sun = vmem(state), vmem(day_t), vmem(sun_t)
    tend, prov_lo = pl.pallas_call(
        functools.partial(first_kernel, rows),
        grid=(steps,),
        in_specs=[in_vmem] * 9,
        out_specs=(pl.BlockSpec((1, rows, cells, feats), lambda i: (0, i, 0, 0)), in_vmem),
        out_shape=(tend_shape, pltpu.VMEM((half, cells, feats), F32)),
        compiler_params=params,
        cost_estimate=pl.CostEstimate(
            flops=2 * half * cells * macs, bytes_accessed=2 * 2**20, transcendentals=0
        ),
        name="nets_first_half",
    )(v_day, v_sun, v_state, *weights)

    def here(i):
        return jnp.minimum(i, steps - 1)

    def before(i):
        return jnp.maximum(i - 1, 0)

    new_state, tend = pl.pallas_call(
        functools.partial(second_kernel, rows),
        grid=(steps + 1,),
        in_specs=[in_vmem] * 7 + [in_hbm] + [in_vmem] * 6,
        out_specs=(
            pl.BlockSpec((2, rows, cells, feats), lambda i: (0, before(i), 0, 0)),
            pl.BlockSpec((1, rows, cells, feats), lambda i: (1, here(i), 0, 0)),
        ),
        out_shape=(jax.ShapeDtypeStruct((2, half, cells, feats), F32), tend_shape),
        input_output_aliases={7: 1},
        scratch_shapes=[
            pltpu.VMEM((rows, cells, feats), F32),
            pltpu.VMEM((4 * rows, feats), F32),
            pltpu.VMEM((2 * rows, levels), F32),
        ],
        compiler_params=params,
        cost_estimate=pl.CostEstimate(
            flops=2 * half * (cells + 4) * macs, bytes_accessed=12 * 2**20, transcendentals=0
        ),
        name="nets_second_half_transport",
    )(v_day, v_sun, v_state, vmem(courant), vmem(halo_a), vmem(halo_b), vmem(prov_lo), tend, *weights)
    return new_state.reshape(state.shape), tend.reshape(state.shape)


def solution(mesh):
    in_specs = (
        P("ens", "lon", None),
        P("ens", "lon", None),
        P("ens", "lon"),
        P("ens", "lon"),
        P(),
        P(),
        P(),
        P(),
        P(),
        P(),
    )
    out_specs = (P("ens", "lon", None), P("ens", "lon", None))
    return jax.shard_map(shards, mesh=mesh, in_specs=in_specs, out_specs=out_specs, check_vma=False)
```

```python
import functools

import jax
import jax.numpy as jnp
from jax import lax
from jax.experimental import pallas as pl
from jax.experimental.pallas import tpu as pltpu
from jax.sharding import PartitionSpec as P

BF16 = jnp.bfloat16
F32 = jnp.float32


def dot(a, b):
    return jnp.dot(a, b, preferred_element_type=F32)


def silu_of_twice(h):
    return (h + h * jnp.tanh(h)).astype(BF16)


def nets(half_cols, sun_col, w):
    long_in, long_out, short_in, short_sun, short_mid, short_out = w
    half_sun = sun_col * 0.5
    sun_row = short_sun[...]
    first = silu_of_twice(dot(half_cols, short_in[...]) + half_sun * sun_row)
    hidden = silu_of_twice(dot(half_cols, long_in[...]))
    second = silu_of_twice(dot(first, short_mid[0]) * 0.5)
    long_tend = dot(hidden, long_out[...])
    third = silu_of_twice(dot(second, short_mid[1]) * 0.5)
    short_tend = dot(third, short_out[...])
    return long_tend + jnp.where(sun_col > 0.0, short_tend, 0.0)


def lit_sun_column(day_ref, sun_ref, row0, rows):
    lit = jnp.where(day_ref[...] > 0, sun_ref[...], 0.0)
    lane = lax.broadcasted_iota(jnp.int32, lit.shape, 1)
    return jnp.concatenate(
        [
            jnp.sum(jnp.where(lane == row0 + r, lit, 0.0), axis=1, keepdims=True)
            for r in range(rows)
        ],
        axis=0,
    )


def pack_kernel(
    day_hbm, sun_hbm, short_sun_hbm, state, courant, out_a, out_b, sun_row,
    day, sun, short_sun, west, east, wind, sems,
):
    feats, levels = state.shape[-1], courant.shape[-1]
    end = feats + levels
    cells, lat_rows = day.shape
    copies = [
        pltpu.make_async_copy(src, dst, sems.at[k])
        for k, (src, dst) in enumerate((
            (state.at[:, pl.ds(0, 1), :], west),
            (state.at[:, pl.ds(cells - 1, 1), :], east),
            (courant.at[:, pl.ds(cells - 1, 1), :], wind),
            (day_hbm, day),
            (sun_hbm, sun),
            (short_sun_hbm, short_sun),
        ))
    ]
    for copy in copies:
        copy.start()
    for copy in copies[3:]:
        copy.wait()
    odd = lax.rem(lax.axis_index("lon"), 2) == 1
    lit = jnp.where(day[...] > 0, sun[...], 0.0)

    def choose(to_east, to_west):
        a, b = jnp.where(odd, to_west, to_east), jnp.where(odd, to_east, to_west)
        return a.astype(BF16), b.astype(BF16)

    sun_row[...] = short_sun[...].astype(F32).reshape(sun_row.shape)
    for out, row in zip((out_a, out_b), choose(lit[cells - 1 :], lit[:1])):
        out[:, end:] = jnp.zeros((lat_rows, out.shape[1] - end), BF16)
        out[:16, end : end + lat_rows] = jnp.broadcast_to(row, (16, lat_rows))
    for copy in copies[:3]:
        copy.wait()
    out_a[:, :feats], out_b[:, :feats] = choose(east[:, 0, :], west[:, 0, :])
    out_a[:, feats:end] = wind[:, 0, :].astype(BF16)
    out_b[:, feats:end] = wind[:, 0, :].astype(BF16)


def first_kernel(rows, day, sun, state, *rest):
    *w, tend, prov = rest
    row0 = pl.multiple_of(pl.program_id(0) * rows, rows)
    _, cells, feats = state.shape
    cols = rows * cells
    sun_col = lit_sun_column(day, sun, row0, rows)
    own = state[pl.ds(row0, rows)].reshape(cols, feats)
    phys = nets((own * 0.5).astype(BF16), sun_col, w)
    tend[0] = phys.astype(BF16).reshape(rows, cells, feats)
    prov[pl.ds(row0, rows)] = (own + phys).reshape(rows, cells, feats)


def transport(prov, courant, west_prov, west_cour, east_prov):
    rows, cells, feats = prov.shape
    cols = rows * cells
    pair = jnp.concatenate([courant, courant], axis=-1)
    east_wind, west_wind = jnp.maximum(pair, 0.0), jnp.minimum(pair, 0.0)
    sub = lax.broadcasted_iota(jnp.int32, (rows, 8, feats), 1)
    nxt = pltpu.roll(prov.reshape(cols, feats), cols - 1, 0).reshape(rows, cells, feats)
    tail = jnp.where(sub == 7, east_prov[:, None, :], nxt[:, cells - 8 :])
    nxt = jnp.concatenate([nxt[:, : cells - 8], tail], axis=1)
    flux = east_wind * prov + west_wind * nxt
    prev = pltpu.roll(flux.reshape(cols, feats), 1, 0).reshape(rows, cells, feats)
    wc = jnp.concatenate([west_cour, west_cour], axis=-1)
    face = (jnp.maximum(wc, 0.0) * west_prov)[:, None, :] + jnp.minimum(wc, 0.0)[:, None, :] * prov[:, :8]
    head = jnp.where(sub == 0, face, prev[:, :8])
    prev = jnp.concatenate([head, prev[:, 8:]], axis=1)
    return prov - (flux - prev)


def second_kernel(
    rows, day, sun, state, courant, halo_a, halo_b, prov_lo, tend_in,
    long_in, long_out, short_in, short_sun, short_mid, short_out,
    new_state, tend, prov, edges, west_wind,
):
    i = pl.program_id(0)
    tiles = pl.num_programs(0) - 1
    half = tiles * rows
    _, cells, feats = state.shape
    cols = rows * cells
    levels = courant.shape[-1]
    end = feats + levels
    lat_rows = day.shape[1]
    odd = lax.rem(lax.axis_index("lon"), 2) == 1

    def column_nets():
        lo = pl.multiple_of(i * rows, rows)
        hi = pl.multiple_of(half + i * rows, rows)

        def sides(at, n, lanes):
            a, b = halo_a[pl.ds(at, n), lanes].astype(F32), halo_b[pl.ds(at, n), lanes].astype(F32)
            return jnp.where(odd, a, b), jnp.where(odd, b, a)

        west_lo, east_lo = sides(lo, rows, slice(0, feats))
        west_hi, east_hi = sides(hi, rows, slice(0, feats))
        halos = [west_lo, west_hi, east_lo, east_hi]
        west_sun, east_sun = sides(0, 16, slice(end, end + 128))
        lane = lax.broadcasted_iota(jnp.int32, (rows, 128), 1)
        sub = lax.broadcasted_iota(jnp.int32, (rows, 128), 0)
        suns = [
            jnp.sum(jnp.where(lane == sub + at, lit, 0.0), axis=1, keepdims=True)
            for lit, at in ((west_sun, lo), (west_sun, hi), (east_sun, lo), (east_sun, hi))
        ]
        sun_all = jnp.concatenate([lit_sun_column(day, sun, hi, rows)] + suns, axis=0)
        own = state[pl.ds(hi, rows)].reshape(cols, feats)
        half_cols = (jnp.concatenate([own] + halos, axis=0) * 0.5).astype(BF16)
        phys = nets(half_cols, sun_all, (long_in, long_out, short_in, short_sun, short_mid, short_out))
        tend[0] = phys[:cols].astype(BF16).reshape(rows, cells, feats)
        prov[...] = (own + phys[:cols]).reshape(rows, cells, feats)
        edges[...] = jnp.concatenate(halos, axis=0) + phys[cols:]
        west_wind[:rows] = sides(lo, rows, slice(feats, end))[0]
        west_wind[rows:] = sides(hi, rows, slice(feats, end))[0]

    def move():
        lo = pl.multiple_of((i - 1) * rows, rows)
        new_state[0] = transport(
            prov_lo[pl.ds(lo, rows)], courant[pl.ds(lo, rows)],
            edges[:rows], west_wind[:rows], edges[2 * rows : 3 * rows],
        )
        new_state[1] = transport(
            prov[...], courant[pl.ds(half + lo, rows)],
            edges[rows : 2 * rows], west_wind[rows:], edges[3 * rows :],
        )

    @pl.when(i == 0)
    def _():
        column_nets()

    @pl.when(jnp.logical_and(i > 0, i < tiles))
    def _():
        move()
        column_nets()

    @pl.when(i == tiles)
    def _():
        move()


def shards(
    state, courant, daylit, insolation, long_in, long_out, short_in, short_sun, short_mid, short_out
):
    lat_rows, cells, feats = state.shape
    levels = courant.shape[-1]
    hid = long_in.shape[1]
    size = lax.axis_size("lon")
    rows = 16
    half = lat_rows // 2
    steps = half // rows
    width = feats + levels + 128
    day_t, sun_t = daylit.T, insolation.T
    in_vmem = pl.BlockSpec(memory_space=pltpu.VMEM)
    in_hbm = pl.BlockSpec(memory_space=pltpu.HBM)
    edge = pltpu.VMEM((lat_rows, width), BF16)
    edge_a, edge_b, sun_row = pl.pallas_call(
        pack_kernel,
        in_specs=[in_hbm] * 5,
        out_specs=(in_vmem,) * 3,
        out_shape=(edge, edge, pltpu.VMEM((1, hid), F32)),
        scratch_shapes=[
            pltpu.VMEM((cells, lat_rows), jnp.int32),
            pltpu.VMEM((cells, lat_rows), F32),
            pltpu.VMEM((hid,), BF16),
            pltpu.VMEM((lat_rows, 1, feats), F32),
            pltpu.VMEM((lat_rows, 1, feats), F32),
            pltpu.VMEM((lat_rows, 1, levels), F32),
            pltpu.SemaphoreType.DMA((6,)),
        ],
        compiler_params=pltpu.CompilerParams(vmem_limit_bytes=8 * 2**20),
        cost_estimate=pl.CostEstimate(flops=8 * 10**9, bytes_accessed=8 * 2**20, transcendentals=0),
        name="edges_packed",
    )(*(pltpu.with_memory_space_constraint(x, pltpu.HBM) for x in (day_t, sun_t, short_sun, state, courant)))
    flip = [(i, i ^ 1) for i in range(size)]
    seam = [(i, (i + 1 if i % 2 else i - 1) % size) for i in range(size)]
    halo_a = lax.ppermute(edge_a, "lon", flip)
    halo_b = lax.ppermute(edge_b, "lon", seam)

    def vmem(x):
        return pltpu.with_memory_space_constraint(x, pltpu.VMEM)

    weights = (vmem(long_in), vmem(long_out), vmem(short_in), sun_row, vmem(short_mid), vmem(short_out))
    macs = 4 * feats * hid + 2 * hid * hid
    params = pltpu.CompilerParams(vmem_limit_bytes=30 * 2**20)
    tend_shape = pltpu.HBM((2, half, cells, feats), BF16)
    v_state, v_day, v_sun = vmem(state), vmem(day_t), vmem(sun_t)
    tend, prov_lo = pl.pallas_call(
        functools.partial(first_kernel, rows),
        grid=(steps,),
        in_specs=[in_vmem] * 9,
        out_specs=(pl.BlockSpec((1, rows, cells, feats), lambda i: (0, i, 0, 0)), in_vmem),
        out_shape=(tend_shape, pltpu.VMEM((half, cells, feats), F32)),
        compiler_params=params,
        cost_estimate=pl.CostEstimate(
            flops=2 * half * cells * macs, bytes_accessed=2 * 2**20, transcendentals=0
        ),
        name="nets_first_half",
    )(v_day, v_sun, v_state, *weights)

    def here(i):
        return jnp.minimum(i, steps - 1)

    def before(i):
        return jnp.maximum(i - 1, 0)

    new_state, tend = pl.pallas_call(
        functools.partial(second_kernel, rows),
        grid=(steps + 1,),
        in_specs=[in_vmem] * 7 + [in_hbm] + [in_vmem] * 6,
        out_specs=(
            pl.BlockSpec((2, rows, cells, feats), lambda i: (0, before(i), 0, 0)),
            pl.BlockSpec((1, rows, cells, feats), lambda i: (1, here(i), 0, 0)),
        ),
        out_shape=(jax.ShapeDtypeStruct((2, half, cells, feats), F32), tend_shape),
        input_output_aliases={7: 1},
        scratch_shapes=[
            pltpu.VMEM((rows, cells, feats), F32),
            pltpu.VMEM((4 * rows, feats), F32),
            pltpu.VMEM((2 * rows, levels), F32),
        ],
        compiler_params=params,
        cost_estimate=pl.CostEstimate(
            flops=2 * half * (cells + 4) * macs, bytes_accessed=12 * 2**20, transcendentals=0
        ),
        name="nets_second_half_transport",
    )(v_day, v_sun, v_state, vmem(courant), vmem(halo_a), vmem(halo_b), vmem(prov_lo), tend, *weights)
    return new_state.reshape(state.shape), tend.reshape(state.shape)


def solution(mesh):
    in_specs = (
        P("ens", "lon", None),
        P("ens", "lon", None),
        P("ens", "lon"),
        P("ens", "lon"),
        P(),
        P(),
        P(),
        P(),
        P(),
        P(),
    )
    out_specs = (P("ens", "lon", None), P("ens", "lon", None))
    return jax.shard_map(shards, mesh=mesh, in_specs=in_specs, out_specs=out_specs, check_vma=False)
```

```python
import functools

import jax
import jax.numpy as jnp
from jax import lax
from jax.experimental import pallas as pl
from jax.experimental.pallas import tpu as pltpu
from jax.sharding import PartitionSpec as P

BF16 = jnp.bfloat16
F32 = jnp.float32


def dot(a, b):
    return jnp.dot(a, b, preferred_element_type=F32)


def silu_of_twice(h):
    return (h + h * jnp.tanh(h)).astype(BF16)


def nets(half_cols, sun_col, w):
    long_in, long_out, short_in, short_sun, short_mid, short_out = w
    half_sun = sun_col * 0.5
    sun_row = short_sun[...]
    first = silu_of_twice(dot(half_cols, short_in[...]) + half_sun * sun_row)
    hidden = silu_of_twice(dot(half_cols, long_in[...]))
    second = silu_of_twice(dot(first, short_mid[0]) * 0.5)
    long_tend = dot(hidden, long_out[...])
    third = silu_of_twice(dot(second, short_mid[1]) * 0.5)
    short_tend = dot(third, short_out[...])
    return long_tend + jnp.where(sun_col > 0.0, short_tend, 0.0)


def lit_sun_column(day_ref, sun_ref, row0, rows):
    lit = jnp.where(day_ref[...] > 0, sun_ref[...], 0.0)
    lane = lax.broadcasted_iota(jnp.int32, lit.shape, 1)
    return jnp.concatenate(
        [
            jnp.sum(jnp.where(lane == row0 + r, lit, 0.0), axis=1, keepdims=True)
            for r in range(rows)
        ],
        axis=0,
    )


def pack_kernel(
    day_hbm, sun_hbm, short_sun_hbm, state, courant, out_b, out_a, sun_row,
    day, sun, short_sun, west, east, wind, sems,
):
    feats, levels = state.shape[-1], courant.shape[-1]
    end = feats + levels
    cells, lat_rows = day.shape
    copies = [
        pltpu.make_async_copy(src, dst, sems.at[k])
        for k, (src, dst) in enumerate((
            (state.at[:, pl.ds(0, 1), :], west),
            (state.at[:, pl.ds(cells - 1, 1), :], east),
            (courant.at[:, pl.ds(cells - 1, 1), :], wind),
            (day_hbm, day),
            (sun_hbm, sun),
            (short_sun_hbm, short_sun),
        ))
    ]
    for copy in copies:
        copy.start()
    for copy in copies[3:]:
        copy.wait()
    odd = lax.rem(lax.axis_index("lon"), 2) == 1
    lit = jnp.where(day[...] > 0, sun[...], 0.0)

    def choose(to_east, to_west):
        a, b = jnp.where(odd, to_west, to_east), jnp.where(odd, to_east, to_west)
        return a.astype(BF16), b.astype(BF16)

    sun_row[...] = short_sun[...].astype(F32).reshape(sun_row.shape)
    for out, row in zip((out_a, out_b), choose(lit[cells - 1 :], lit[:1])):
        out[:, end:] = jnp.zeros((lat_rows, out.shape[1] - end), BF16)
        out[:16, end : end + lat_rows] = jnp.broadcast_to(row, (16, lat_rows))
    for copy in copies[:3]:
        copy.wait()
    out_a[:, :feats], out_b[:, :feats] = choose(east[:, 0, :], west[:, 0, :])
    out_a[:, feats:end] = wind[:, 0, :].astype(BF16)
    out_b[:, feats:end] = wind[:, 0, :].astype(BF16)


def first_kernel(rows, day, sun, state, *rest):
    *w, tend, prov = rest
    row0 = pl.multiple_of(pl.program_id(0) * rows, rows)
    _, cells, feats = state.shape
    cols = rows * cells
    sun_col = lit_sun_column(day, sun, row0, rows)
    own = state[pl.ds(row0, rows)].reshape(cols, feats)
    phys = nets((own * 0.5).astype(BF16), sun_col, w)
    tend[0] = phys.astype(BF16).reshape(rows, cells, feats)
    prov[pl.ds(row0, rows)] = (own + phys).reshape(rows, cells, feats)


def transport(prov, courant, west_prov, west_cour, east_prov):
    rows, cells, feats = prov.shape
    cols = rows * cells
    pair = jnp.concatenate([courant, courant], axis=-1)
    east_wind, west_wind = jnp.maximum(pair, 0.0), jnp.minimum(pair, 0.0)
    sub = lax.broadcasted_iota(jnp.int32, (rows, 8, feats), 1)
    nxt = pltpu.roll(prov.reshape(cols, feats), cols - 1, 0).reshape(rows, cells, feats)
    tail = jnp.where(sub == 7, east_prov[:, None, :], nxt[:, cells - 8 :])
    nxt = jnp.concatenate([nxt[:, : cells - 8], tail], axis=1)
    flux = east_wind * prov + west_wind * nxt
    prev = pltpu.roll(flux.reshape(cols, feats), 1, 0).reshape(rows, cells, feats)
    wc = jnp.concatenate([west_cour, west_cour], axis=-1)
    face = (jnp.maximum(wc, 0.0) * west_prov)[:, None, :] + jnp.minimum(wc, 0.0)[:, None, :] * prov[:, :8]
    head = jnp.where(sub == 0, face, prev[:, :8])
    prev = jnp.concatenate([head, prev[:, 8:]], axis=1)
    return prov - (flux - prev)


def second_kernel(
    rows, day, sun, state, courant, halo_b, halo_a, prov_lo, tend_in,
    long_in, long_out, short_in, short_sun, short_mid, short_out,
    new_state, tend, prov, edges, west_wind,
):
    i = pl.program_id(0)
    tiles = pl.num_programs(0) - 1
    half = tiles * rows
    _, cells, feats = state.shape
    cols = rows * cells
    levels = courant.shape[-1]
    end = feats + levels
    lat_rows = day.shape[1]
    odd = lax.rem(lax.axis_index("lon"), 2) == 1

    def column_nets():
        lo = pl.multiple_of(i * rows, rows)
        hi = pl.multiple_of(half + i * rows, rows)

        def sides(at, n, lanes):
            a, b = halo_a[pl.ds(at, n), lanes].astype(F32), halo_b[pl.ds(at, n), lanes].astype(F32)
            return jnp.where(odd, a, b), jnp.where(odd, b, a)

        west_lo, east_lo = sides(lo, rows, slice(0, feats))
        west_hi, east_hi = sides(hi, rows, slice(0, feats))
        halos = [west_lo, west_hi, east_lo, east_hi]
        west_sun, east_sun = sides(0, 16, slice(end, end + 128))
        lane = lax.broadcasted_iota(jnp.int32, (rows, 128), 1)
        sub = lax.broadcasted_iota(jnp.int32, (rows, 128), 0)
        suns = [
            jnp.sum(jnp.where(lane == sub + at, lit, 0.0), axis=1, keepdims=True)
            for lit, at in ((west_sun, lo), (west_sun, hi), (east_sun, lo), (east_sun, hi))
        ]
        sun_all = jnp.concatenate([lit_sun_column(day, sun, hi, rows)] + suns, axis=0)
        own = state[pl.ds(hi, rows)].reshape(cols, feats)
        half_cols = (jnp.concatenate([own] + halos, axis=0) * 0.5).astype(BF16)
        phys = nets(half_cols, sun_all, (long_in, long_out, short_in, short_sun, short_mid, short_out))
        tend[0] = phys[:cols].astype(BF16).reshape(rows, cells, feats)
        prov[...] = (own + phys[:cols]).reshape(rows, cells, feats)
        edges[...] = jnp.concatenate(halos, axis=0) + phys[cols:]
        west_wind[:rows] = sides(lo, rows, slice(feats, end))[0]
        west_wind[rows:] = sides(hi, rows, slice(feats, end))[0]

    def move():
        lo = pl.multiple_of((i - 1) * rows, rows)
        new_state[0] = transport(
            prov_lo[pl.ds(lo, rows)], courant[pl.ds(lo, rows)],
            edges[:rows], west_wind[:rows], edges[2 * rows : 3 * rows],
        )
        new_state[1] = transport(
            prov[...], courant[pl.ds(half + lo, rows)],
            edges[rows : 2 * rows], west_wind[rows:], edges[3 * rows :],
        )

    @pl.when(i == 0)
    def _():
        column_nets()

    @pl.when(jnp.logical_and(i > 0, i < tiles))
    def _():
        move()
        column_nets()

    @pl.when(i == tiles)
    def _():
        move()


def shards(
    state, courant, daylit, insolation, long_in, long_out, short_in, short_sun, short_mid, short_out
):
    lat_rows, cells, feats = state.shape
    levels = courant.shape[-1]
    hid = long_in.shape[1]
    size = lax.axis_size("lon")
    rows = 16
    half = lat_rows // 2
    steps = half // rows
    width = feats + levels + 128
    day_t, sun_t = daylit.T, insolation.T
    in_vmem = pl.BlockSpec(memory_space=pltpu.VMEM)
    in_hbm = pl.BlockSpec(memory_space=pltpu.HBM)
    edge = pltpu.VMEM((lat_rows, width), BF16)
    edge_b, edge_a, sun_row = pl.pallas_call(
        pack_kernel,
        in_specs=[in_hbm] * 5,
        out_specs=(in_vmem,) * 3,
        out_shape=(edge, edge, pltpu.VMEM((1, hid), F32)),
        scratch_shapes=[
            pltpu.VMEM((cells, lat_rows), jnp.int32),
            pltpu.VMEM((cells, lat_rows), F32),
            pltpu.VMEM((hid,), BF16),
            pltpu.VMEM((lat_rows, 1, feats), F32),
            pltpu.VMEM((lat_rows, 1, feats), F32),
            pltpu.VMEM((lat_rows, 1, levels), F32),
            pltpu.SemaphoreType.DMA((6,)),
        ],
        compiler_params=pltpu.CompilerParams(vmem_limit_bytes=8 * 2**20),
        cost_estimate=pl.CostEstimate(flops=8 * 10**9, bytes_accessed=8 * 2**20, transcendentals=0),
        name="edges_packed",
    )(*(pltpu.with_memory_space_constraint(x, pltpu.HBM) for x in (day_t, sun_t, short_sun, state, courant)))
    flip = [(i, i ^ 1) for i in range(size)]
    seam = [(i, (i + 1 if i % 2 else i - 1) % size) for i in range(size)]
    halo_b = lax.ppermute(edge_b, "lon", seam)
    halo_a = lax.ppermute(edge_a, "lon", flip)

    def vmem(x):
        return pltpu.with_memory_space_constraint(x, pltpu.VMEM)

    weights = (vmem(long_in), vmem(long_out), vmem(short_in), sun_row, vmem(short_mid), vmem(short_out))
    macs = 4 * feats * hid + 2 * hid * hid
    params = pltpu.CompilerParams(vmem_limit_bytes=30 * 2**20)
    tend_shape = pltpu.HBM((2, half, cells, feats), BF16)
    v_state, v_day, v_sun = vmem(state), vmem(day_t), vmem(sun_t)
    tend, prov_lo = pl.pallas_call(
        functools.partial(first_kernel, rows),
        grid=(steps,),
        in_specs=[in_vmem] * 9,
        out_specs=(pl.BlockSpec((1, rows, cells, feats), lambda i: (0, i, 0, 0)), in_vmem),
        out_shape=(tend_shape, pltpu.VMEM((half, cells, feats), F32)),
        compiler_params=params,
        cost_estimate=pl.CostEstimate(
            flops=2 * half * cells * macs, bytes_accessed=2 * 2**20, transcendentals=0
        ),
        name="nets_first_half",
    )(v_day, v_sun, v_state, *weights)

    def here(i):
        return jnp.minimum(i, steps - 1)

    def before(i):
        return jnp.maximum(i - 1, 0)

    new_state, tend = pl.pallas_call(
        functools.partial(second_kernel, rows),
        grid=(steps + 1,),
        in_specs=[in_vmem] * 7 + [in_hbm] + [in_vmem] * 6,
        out_specs=(
            pl.BlockSpec((2, rows, cells, feats), lambda i: (0, before(i), 0, 0)),
            pl.BlockSpec((1, rows, cells, feats), lambda i: (1, here(i), 0, 0)),
        ),
        out_shape=(jax.ShapeDtypeStruct((2, half, cells, feats), F32), tend_shape),
        input_output_aliases={7: 1},
        scratch_shapes=[
            pltpu.VMEM((rows, cells, feats), F32),
            pltpu.VMEM((4 * rows, feats), F32),
            pltpu.VMEM((2 * rows, levels), F32),
        ],
        compiler_params=params,
        cost_estimate=pl.CostEstimate(
            flops=2 * half * (cells + 4) * macs, bytes_accessed=12 * 2**20, transcendentals=0
        ),
        name="nets_second_half_transport",
    )(v_day, v_sun, v_state, vmem(courant), vmem(halo_b), vmem(halo_a), vmem(prov_lo), tend, *weights)
    return new_state.reshape(state.shape), tend.reshape(state.shape)


def solution(mesh):
    in_specs = (
        P("ens", "lon", None),
        P("ens", "lon", None),
        P("ens", "lon"),
        P("ens", "lon"),
        P(),
        P(),
        P(),
        P(),
        P(),
        P(),
    )
    out_specs = (P("ens", "lon", None), P("ens", "lon", None))
    return jax.shard_map(shards, mesh=mesh, in_specs=in_specs, out_specs=out_specs, check_vma=False)
```

```python
import functools

import jax
import jax.numpy as jnp
from jax import lax
from jax.experimental import pallas as pl
from jax.experimental.pallas import tpu as pltpu
from jax.sharding import PartitionSpec as P

BF16 = jnp.bfloat16
F32 = jnp.float32


def dot(a, b):
    return jnp.dot(a, b, preferred_element_type=F32)


def silu_of_twice(h):
    return (h + h * jnp.tanh(h)).astype(BF16)


def nets(half_cols, sun_col, w):
    long_in, long_out, short_in, short_sun, short_mid, short_out = w
    half_sun = sun_col * 0.5
    sun_row = short_sun[...]
    first = silu_of_twice(dot(half_cols, short_in[...]) + half_sun * sun_row)
    hidden = silu_of_twice(dot(half_cols, long_in[...]))
    second = silu_of_twice(dot(first, short_mid[0]) * 0.5)
    long_tend = dot(hidden, long_out[...])
    third = silu_of_twice(dot(second, short_mid[1]) * 0.5)
    short_tend = dot(third, short_out[...])
    return long_tend + jnp.where(sun_col > 0.0, short_tend, 0.0)


def lit_sun_column(day_ref, sun_ref, row0, rows):
    lit = jnp.where(day_ref[...] > 0, sun_ref[...], 0.0)
    lane = lax.broadcasted_iota(jnp.int32, lit.shape, 1)
    return jnp.concatenate(
        [
            jnp.sum(jnp.where(lane == row0 + r, lit, 0.0), axis=1, keepdims=True)
            for r in range(rows)
        ],
        axis=0,
    )


def pack_kernel(
    day_hbm, sun_hbm, short_sun_hbm, state, courant, out_b, out_a, sun_row,
    day, sun, short_sun, west, east, wind, sems,
):
    feats, levels = state.shape[-1], courant.shape[-1]
    end = feats + levels
    cells, lat_rows = day.shape
    copies = [
        pltpu.make_async_copy(src, dst, sems.at[k])
        for k, (src, dst) in enumerate((
            (state.at[:, pl.ds(0, 1), :], west),
            (state.at[:, pl.ds(cells - 1, 1), :], east),
            (courant.at[:, pl.ds(cells - 1, 1), :], wind),
            (day_hbm, day),
            (sun_hbm, sun),
            (short_sun_hbm, short_sun),
        ))
    ]
    for copy in copies:
        copy.start()
    for copy in copies[3:]:
        copy.wait()
    odd = lax.rem(lax.axis_index("lon"), 2) == 1
    lit = jnp.where(day[...] > 0, sun[...], 0.0)

    def choose(to_east, to_west):
        a, b = jnp.where(odd, to_west, to_east), jnp.where(odd, to_east, to_west)
        return a.astype(BF16), b.astype(BF16)

    sun_row[...] = short_sun[...].astype(F32).reshape(sun_row.shape)
    for out, row in zip((out_a, out_b), choose(lit[cells - 1 :], lit[:1])):
        out[:, end:] = jnp.zeros((lat_rows, out.shape[1] - end), BF16)
        out[:16, end : end + lat_rows] = jnp.broadcast_to(row, (16, lat_rows))
    for copy in copies[:3]:
        copy.wait()
    out_a[:, :feats], out_b[:, :feats] = choose(east[:, 0, :], west[:, 0, :])
    out_a[:, feats:end] = wind[:, 0, :].astype(BF16)
    out_b[:, feats:end] = wind[:, 0, :].astype(BF16)


def first_kernel(rows, day, sun, state, *rest):
    *w, tend, prov = rest
    row0 = pl.multiple_of(pl.program_id(0) * rows, rows)
    _, cells, feats = state.shape
    cols = rows * cells
    sun_col = lit_sun_column(day, sun, row0, rows)
    own = state[pl.ds(row0, rows)].reshape(cols, feats)
    phys = nets((own * 0.5).astype(BF16), sun_col, w)
    tend[0] = phys.astype(BF16).reshape(rows, cells, feats)
    prov[pl.ds(row0, rows)] = (own + phys).reshape(rows, cells, feats)


def transport(prov, courant, west_prov, west_cour, east_prov):
    rows, cells, feats = prov.shape
    cols = rows * cells
    levels = courant.shape[-1]
    eastward = courant > 0.0

    def upwind(wind, mask, here, there):
        return jnp.concatenate(
            [wind * jnp.where(mask, here[..., k : k + levels], there[..., k : k + levels]) for k in (0, levels)], axis=-1
        )

    sub = lax.broadcasted_iota(jnp.int32, (rows, 8, feats), 1)
    nxt = pltpu.roll(prov.reshape(cols, feats), cols - 1, 0).reshape(rows, cells, feats)
    tail = jnp.where(sub == 7, east_prov[:, None, :], nxt[:, cells - 8 :])
    nxt = jnp.concatenate([nxt[:, : cells - 8], tail], axis=1)
    flux = upwind(courant, eastward, prov, nxt)
    prev = pltpu.roll(flux.reshape(cols, feats), 1, 0).reshape(rows, cells, feats)
    west_wind = jnp.broadcast_to(west_cour[:, None, :], (rows, 8, levels))
    west_here = jnp.broadcast_to(west_prov[:, None, :], (rows, 8, feats))
    face = upwind(west_wind, west_wind > 0.0, west_here, prov[:, :8])
    head = jnp.where(sub == 0, face, prev[:, :8])
    prev = jnp.concatenate([head, prev[:, 8:]], axis=1)
    return prov - (flux - prev)


def second_kernel(
    rows, day, sun, state, courant, halo_b, halo_a, prov_lo, tend_in,
    long_in, long_out, short_in, short_sun, short_mid, short_out,
    new_state, tend, prov, edges, west_wind,
):
    i = pl.program_id(0)
    tiles = pl.num_programs(0) - 1
    half = tiles * rows
    _, cells, feats = state.shape
    cols = rows * cells
    levels = courant.shape[-1]
    end = feats + levels
    lat_rows = day.shape[1]
    odd = lax.rem(lax.axis_index("lon"), 2) == 1

    def column_nets():
        lo = pl.multiple_of(i * rows, rows)
        hi = pl.multiple_of(half + i * rows, rows)

        def sides(at, n, lanes):
            a, b = halo_a[pl.ds(at, n), lanes].astype(F32), halo_b[pl.ds(at, n), lanes].astype(F32)
            return jnp.where(odd, a, b), jnp.where(odd, b, a)

        west_lo, east_lo = sides(lo, rows, slice(0, feats))
        west_hi, east_hi = sides(hi, rows, slice(0, feats))
        halos = [west_lo, west_hi, east_lo, east_hi]
        west_sun, east_sun = sides(0, 16, slice(end, end + 128))
        lane = lax.broadcasted_iota(jnp.int32, (rows, 128), 1)
        sub = lax.broadcasted_iota(jnp.int32, (rows, 128), 0)
        suns = [
            jnp.sum(jnp.where(lane == sub + at, lit, 0.0), axis=1, keepdims=True)
            for lit, at in ((west_sun, lo), (west_sun, hi), (east_sun, lo), (east_sun, hi))
        ]
        sun_all = jnp.concatenate([lit_sun_column(day, sun, hi, rows)] + suns, axis=0)
        own = state[pl.ds(hi, rows)].reshape(cols, feats)
        half_cols = (jnp.concatenate([own] + halos, axis=0) * 0.5).astype(BF16)
        phys = nets(half_cols, sun_all, (long_in, long_out, short_in, short_sun, short_mid, short_out))
        tend[0] = phys[:cols].astype(BF16).reshape(rows, cells, feats)
        prov[...] = (own + phys[:cols]).reshape(rows, cells, feats)
        edges[...] = jnp.concatenate(halos, axis=0) + phys[cols:]
        west_wind[:rows] = sides(lo, rows, slice(feats, end))[0]
        west_wind[rows:] = sides(hi, rows, slice(feats, end))[0]

    def move():
        lo = pl.multiple_of((i - 1) * rows, rows)
        new_state[0] = transport(
            prov_lo[pl.ds(lo, rows)], courant[pl.ds(lo, rows)],
            edges[:rows], west_wind[:rows], edges[2 * rows : 3 * rows],
        )
        new_state[1] = transport(
            prov[...], courant[pl.ds(half + lo, rows)],
            edges[rows : 2 * rows], west_wind[rows:], edges[3 * rows :],
        )

    @pl.when(i == 0)
    def _():
        column_nets()

    @pl.when(jnp.logical_and(i > 0, i < tiles))
    def _():
        move()
        column_nets()

    @pl.when(i == tiles)
    def _():
        move()


def shards(
    state, courant, daylit, insolation, long_in, long_out, short_in, short_sun, short_mid, short_out
):
    lat_rows, cells, feats = state.shape
    levels = courant.shape[-1]
    hid = long_in.shape[1]
    size = lax.axis_size("lon")
    rows = 16
    half = lat_rows // 2
    steps = half // rows
    width = feats + levels + 128
    day_t, sun_t = daylit.T, insolation.T
    in_vmem = pl.BlockSpec(memory_space=pltpu.VMEM)
    in_hbm = pl.BlockSpec(memory_space=pltpu.HBM)
    edge = pltpu.VMEM((lat_rows, width), BF16)
    edge_b, edge_a, sun_row = pl.pallas_call(
        pack_kernel,
        in_specs=[in_hbm] * 5,
        out_specs=(in_vmem,) * 3,
        out_shape=(edge, edge, pltpu.VMEM((1, hid), F32)),
        scratch_shapes=[
            pltpu.VMEM((cells, lat_rows), jnp.int32),
            pltpu.VMEM((cells, lat_rows), F32),
            pltpu.VMEM((hid,), BF16),
            pltpu.VMEM((lat_rows, 1, feats), F32),
            pltpu.VMEM((lat_rows, 1, feats), F32),
            pltpu.VMEM((lat_rows, 1, levels), F32),
            pltpu.SemaphoreType.DMA((6,)),
        ],
        compiler_params=pltpu.CompilerParams(vmem_limit_bytes=8 * 2**20),
        cost_estimate=pl.CostEstimate(flops=8 * 10**9, bytes_accessed=8 * 2**20, transcendentals=0),
        name="edges_packed",
    )(*(pltpu.with_memory_space_constraint(x, pltpu.HBM) for x in (day_t, sun_t, short_sun, state, courant)))
    flip = [(i, i ^ 1) for i in range(size)]
    seam = [(i, (i + 1 if i % 2 else i - 1) % size) for i in range(size)]
    halo_b = lax.ppermute(edge_b, "lon", seam)
    halo_a = lax.ppermute(edge_a, "lon", flip)

    def vmem(x):
        return pltpu.with_memory_space_constraint(x, pltpu.VMEM)

    weights = (vmem(long_in), vmem(long_out), vmem(short_in), sun_row, vmem(short_mid), vmem(short_out))
    macs = 4 * feats * hid + 2 * hid * hid
    params = pltpu.CompilerParams(vmem_limit_bytes=30 * 2**20)
    tend_shape = pltpu.HBM((2, half, cells, feats), BF16)
    v_state, v_day, v_sun = vmem(state), vmem(day_t), vmem(sun_t)
    tend, prov_lo = pl.pallas_call(
        functools.partial(first_kernel, rows),
        grid=(steps,),
        in_specs=[in_vmem] * 9,
        out_specs=(pl.BlockSpec((1, rows, cells, feats), lambda i: (0, i, 0, 0)), in_vmem),
        out_shape=(tend_shape, pltpu.VMEM((half, cells, feats), F32)),
        compiler_params=params,
        cost_estimate=pl.CostEstimate(
            flops=2 * half * cells * macs, bytes_accessed=2 * 2**20, transcendentals=0
        ),
        name="nets_first_half",
    )(v_day, v_sun, v_state, *weights)

    def here(i):
        return jnp.minimum(i, steps - 1)

    def before(i):
        return jnp.maximum(i - 1, 0)

    new_state, tend = pl.pallas_call(
        functools.partial(second_kernel, rows),
        grid=(steps + 1,),
        in_specs=[in_vmem] * 7 + [in_hbm] + [in_vmem] * 6,
        out_specs=(
            pl.BlockSpec((2, rows, cells, feats), lambda i: (0, before(i), 0, 0)),
            pl.BlockSpec((1, rows, cells, feats), lambda i: (1, here(i), 0, 0)),
        ),
        out_shape=(jax.ShapeDtypeStruct((2, half, cells, feats), F32), tend_shape),
        input_output_aliases={7: 1},
        scratch_shapes=[
            pltpu.VMEM((rows, cells, feats), F32),
            pltpu.VMEM((4 * rows, feats), F32),
            pltpu.VMEM((2 * rows, levels), F32),
        ],
        compiler_params=params,
        cost_estimate=pl.CostEstimate(
            flops=2 * half * (cells + 4) * macs, bytes_accessed=12 * 2**20, transcendentals=0
        ),
        name="nets_second_half_transport",
    )(v_day, v_sun, v_state, vmem(courant), vmem(halo_b), vmem(halo_a), vmem(prov_lo), tend, *weights)
    return new_state.reshape(state.shape), tend.reshape(state.shape)


def solution(mesh):
    in_specs = (
        P("ens", "lon", None),
        P("ens", "lon", None),
        P("ens", "lon"),
        P("ens", "lon"),
        P(),
        P(),
        P(),
        P(),
        P(),
        P(),
    )
    out_specs = (P("ens", "lon", None), P("ens", "lon", None))
    return jax.shard_map(shards, mesh=mesh, in_specs=in_specs, out_specs=out_specs, check_vma=False)
```

```python
import functools

import jax
import jax.numpy as jnp
from jax import lax
from jax.experimental import pallas as pl
from jax.experimental.pallas import tpu as pltpu
from jax.sharding import PartitionSpec as P

BF16 = jnp.bfloat16
F32 = jnp.float32


def dot(a, b):
    return jnp.dot(a, b, preferred_element_type=F32)


def silu_of_twice(h):
    return (h + h * jnp.tanh(h)).astype(BF16)


def nets(half_cols, sun_col, w):
    long_in, long_out, short_in, short_sun, short_mid, short_out = w
    half_sun = sun_col * 0.5
    sun_row = short_sun[...]
    first = silu_of_twice(dot(half_cols, short_in[...]) + half_sun * sun_row)
    hidden = silu_of_twice(dot(half_cols, long_in[...]))
    second = silu_of_twice(dot(first, short_mid[0]) * 0.5)
    long_tend = dot(hidden, long_out[...])
    third = silu_of_twice(dot(second, short_mid[1]) * 0.5)
    short_tend = dot(third, short_out[...])
    return long_tend + jnp.where(sun_col > 0.0, short_tend, 0.0)


def lit_sun_column(day_ref, sun_ref, row0, rows):
    lit = jnp.where(day_ref[...] > 0, sun_ref[...], 0.0)
    lane = lax.broadcasted_iota(jnp.int32, lit.shape, 1)
    return jnp.concatenate(
        [
            jnp.sum(jnp.where(lane == row0 + r, lit, 0.0), axis=1, keepdims=True)
            for r in range(rows)
        ],
        axis=0,
    )


def pack_kernel(
    day_hbm, sun_hbm, short_sun_hbm, state, courant, out_b, out_a, sun_row,
    day, sun, short_sun, west, east, wind, sems,
):
    feats, levels = state.shape[-1], courant.shape[-1]
    end = feats + levels
    cells, lat_rows = day.shape
    copies = [
        pltpu.make_async_copy(src, dst, sems.at[k])
        for k, (src, dst) in enumerate((
            (state.at[:, pl.ds(0, 1), :], west),
            (state.at[:, pl.ds(cells - 1, 1), :], east),
            (courant.at[:, pl.ds(cells - 1, 1), :], wind),
            (day_hbm, day),
            (sun_hbm, sun),
            (short_sun_hbm, short_sun),
        ))
    ]
    for copy in copies:
        copy.start()
    for copy in copies[3:]:
        copy.wait()
    odd = lax.rem(lax.axis_index("lon"), 2) == 1
    lit = jnp.where(day[...] > 0, sun[...], 0.0)

    def choose(to_east, to_west):
        a, b = jnp.where(odd, to_west, to_east), jnp.where(odd, to_east, to_west)
        return a.astype(BF16), b.astype(BF16)

    sun_row[...] = short_sun[...].astype(F32).reshape(sun_row.shape)
    for out, row in zip((out_a, out_b), choose(lit[cells - 1 :], lit[:1])):
        out[:, end:] = jnp.zeros((lat_rows, out.shape[1] - end), BF16)
        out[:16, end : end + lat_rows] = jnp.broadcast_to(row, (16, lat_rows))
    for copy in copies[:3]:
        copy.wait()
    out_a[:, :feats], out_b[:, :feats] = choose(east[:, 0, :], west[:, 0, :])
    out_a[:, feats:end] = wind[:, 0, :].astype(BF16)
    out_b[:, feats:end] = wind[:, 0, :].astype(BF16)


def first_kernel(rows, day, sun, state, *rest):
    *w, tend, prov = rest
    row0 = pl.multiple_of(pl.program_id(0) * rows, rows)
    _, cells, feats = state.shape
    cols = rows * cells
    sun_col = lit_sun_column(day, sun, row0, rows)
    own = state[pl.ds(row0, rows)].reshape(cols, feats)
    phys = nets((own * 0.5).astype(BF16), sun_col, w)
    tend[0] = phys.astype(BF16).reshape(rows, cells, feats)
    prov[pl.ds(row0, rows)] = (own + phys).reshape(rows, cells, feats)


def transport(prov, courant, west_prov, west_cour, east_prov):
    rows, cells, feats = prov.shape
    cols = rows * cells
    levels = courant.shape[-1]
    eastward = courant > 0.0

    def upwind(wind, mask, here, there):
        return jnp.concatenate(
            [wind * jnp.where(mask, here[..., k : k + levels], there[..., k : k + levels]) for k in (0, levels)], axis=-1
        )

    sub = lax.broadcasted_iota(jnp.int32, (rows, 8, feats), 1)
    nxt = pltpu.roll(prov.reshape(cols, feats), cols - 1, 0).reshape(rows, cells, feats)
    tail = jnp.where(sub == 7, east_prov[:, None, :], nxt[:, cells - 8 :])
    nxt = jnp.concatenate([nxt[:, : cells - 8], tail], axis=1)
    flux = upwind(courant, eastward, prov, nxt)
    prev = pltpu.roll(flux.reshape(cols, feats), 1, 0).reshape(rows, cells, feats)
    west_wind = jnp.broadcast_to(west_cour[:, None, :], (rows, 8, levels))
    west_here = jnp.broadcast_to(west_prov[:, None, :], (rows, 8, feats))
    face = upwind(west_wind, west_wind > 0.0, west_here, prov[:, :8])
    head = jnp.where(sub == 0, face, prev[:, :8])
    prev = jnp.concatenate([head, prev[:, 8:]], axis=1)
    return prov - (flux - prev)


def second_kernel(
    rows, day, sun, state, courant, halo_b, halo_a, prov_lo, tend_in,
    long_in, long_out, short_in, short_sun, short_mid, short_out,
    new_state, tend, prov, edges, west_wind,
):
    i = pl.program_id(0)
    tiles = pl.num_programs(0)
    half = tiles * rows
    _, cells, feats = state.shape
    cols = rows * cells
    levels = courant.shape[-1]
    end = feats + levels
    lat_rows = day.shape[1]
    odd = lax.rem(lax.axis_index("lon"), 2) == 1

    def column_nets():
        lo = pl.multiple_of(i * rows, rows)
        hi = pl.multiple_of(half + i * rows, rows)

        def sides(at, n, lanes):
            a, b = halo_a[pl.ds(at, n), lanes].astype(F32), halo_b[pl.ds(at, n), lanes].astype(F32)
            return jnp.where(odd, a, b), jnp.where(odd, b, a)

        west_lo, east_lo = sides(lo, rows, slice(0, feats))
        west_hi, east_hi = sides(hi, rows, slice(0, feats))
        halos = [west_lo, west_hi, east_lo, east_hi]
        west_sun, east_sun = sides(0, 16, slice(end, end + 128))
        lane = lax.broadcasted_iota(jnp.int32, (rows, 128), 1)
        sub = lax.broadcasted_iota(jnp.int32, (rows, 128), 0)
        suns = [
            jnp.sum(jnp.where(lane == sub + at, lit, 0.0), axis=1, keepdims=True)
            for lit, at in ((west_sun, lo), (west_sun, hi), (east_sun, lo), (east_sun, hi))
        ]
        sun_all = jnp.concatenate([lit_sun_column(day, sun, hi, rows)] + suns, axis=0)
        own = state[pl.ds(hi, rows)].reshape(cols, feats)
        half_cols = (jnp.concatenate([own] + halos, axis=0) * 0.5).astype(BF16)
        phys = nets(half_cols, sun_all, (long_in, long_out, short_in, short_sun, short_mid, short_out))
        tend[0] = phys[:cols].astype(BF16).reshape(rows, cells, feats)
        prov[...] = (own + phys[:cols]).reshape(rows, cells, feats)
        edges[...] = jnp.concatenate(halos, axis=0) + phys[cols:]
        west_wind[:rows] = sides(lo, rows, slice(feats, end))[0]
        west_wind[rows:] = sides(hi, rows, slice(feats, end))[0]

    def move():
        lo = pl.multiple_of(i * rows, rows)
        new_state[0] = transport(
            prov_lo[pl.ds(lo, rows)], courant[pl.ds(lo, rows)],
            edges[:rows], west_wind[:rows], edges[2 * rows : 3 * rows],
        )
        new_state[1] = transport(
            prov[...], courant[pl.ds(half + lo, rows)],
            edges[rows : 2 * rows], west_wind[rows:], edges[3 * rows :],
        )

    column_nets()
    move()


def shards(
    state, courant, daylit, insolation, long_in, long_out, short_in, short_sun, short_mid, short_out
):
    lat_rows, cells, feats = state.shape
    levels = courant.shape[-1]
    hid = long_in.shape[1]
    size = lax.axis_size("lon")
    rows = 16
    half = lat_rows // 2
    steps = half // rows
    width = feats + levels + 128
    day_t, sun_t = daylit.T, insolation.T
    in_vmem = pl.BlockSpec(memory_space=pltpu.VMEM)
    in_hbm = pl.BlockSpec(memory_space=pltpu.HBM)
    edge = pltpu.VMEM((lat_rows, width), BF16)
    edge_b, edge_a, sun_row = pl.pallas_call(
        pack_kernel,
        in_specs=[in_hbm] * 5,
        out_specs=(in_vmem,) * 3,
        out_shape=(edge, edge, pltpu.VMEM((1, hid), F32)),
        scratch_shapes=[
            pltpu.VMEM((cells, lat_rows), jnp.int32),
            pltpu.VMEM((cells, lat_rows), F32),
            pltpu.VMEM((hid,), BF16),
            pltpu.VMEM((lat_rows, 1, feats), F32),
            pltpu.VMEM((lat_rows, 1, feats), F32),
            pltpu.VMEM((lat_rows, 1, levels), F32),
            pltpu.SemaphoreType.DMA((6,)),
        ],
        compiler_params=pltpu.CompilerParams(vmem_limit_bytes=8 * 2**20),
        cost_estimate=pl.CostEstimate(flops=8 * 10**9, bytes_accessed=8 * 2**20, transcendentals=0),
        name="edges_packed",
    )(*(pltpu.with_memory_space_constraint(x, pltpu.HBM) for x in (day_t, sun_t, short_sun, state, courant)))
    flip = [(i, i ^ 1) for i in range(size)]
    seam = [(i, (i + 1 if i % 2 else i - 1) % size) for i in range(size)]
    halo_b = lax.ppermute(edge_b, "lon", seam)
    halo_a = lax.ppermute(edge_a, "lon", flip)

    def vmem(x):
        return pltpu.with_memory_space_constraint(x, pltpu.VMEM)

    weights = (vmem(long_in), vmem(long_out), vmem(short_in), sun_row, vmem(short_mid), vmem(short_out))
    macs = 4 * feats * hid + 2 * hid * hid
    params = pltpu.CompilerParams(vmem_limit_bytes=30 * 2**20)
    tend_shape = pltpu.HBM((2, half, cells, feats), BF16)
    v_state, v_day, v_sun = vmem(state), vmem(day_t), vmem(sun_t)
    tend, prov_lo = pl.pallas_call(
        functools.partial(first_kernel, rows),
        grid=(steps,),
        in_specs=[in_vmem] * 9,
        out_specs=(pl.BlockSpec((1, rows, cells, feats), lambda i: (0, i, 0, 0)), in_vmem),
        out_shape=(tend_shape, pltpu.VMEM((half, cells, feats), F32)),
        compiler_params=params,
        cost_estimate=pl.CostEstimate(
            flops=2 * half * cells * macs, bytes_accessed=2 * 2**20, transcendentals=0
        ),
        name="nets_first_half",
    )(v_day, v_sun, v_state, *weights)

    new_state, tend = pl.pallas_call(
        functools.partial(second_kernel, rows),
        grid=(steps,),
        in_specs=[in_vmem] * 7 + [in_hbm] + [in_vmem] * 6,
        out_specs=(
            pl.BlockSpec((2, rows, cells, feats), lambda i: (0, i, 0, 0)),
            pl.BlockSpec((1, rows, cells, feats), lambda i: (1, i, 0, 0)),
        ),
        out_shape=(jax.ShapeDtypeStruct((2, half, cells, feats), F32), tend_shape),
        input_output_aliases={7: 1},
        scratch_shapes=[
            pltpu.VMEM((rows, cells, feats), F32),
            pltpu.VMEM((4 * rows, feats), F32),
            pltpu.VMEM((2 * rows, levels), F32),
        ],
        compiler_params=params,
        cost_estimate=pl.CostEstimate(
            flops=2 * half * (cells + 4) * macs, bytes_accessed=12 * 2**20, transcendentals=0
        ),
        name="nets_second_half_transport",
    )(v_day, v_sun, v_state, vmem(courant), vmem(halo_b), vmem(halo_a), vmem(prov_lo), tend, *weights)
    return new_state.reshape(state.shape), tend.reshape(state.shape)


def solution(mesh):
    in_specs = (
        P("ens", "lon", None),
        P("ens", "lon", None),
        P("ens", "lon"),
        P("ens", "lon"),
        P(),
        P(),
        P(),
        P(),
        P(),
        P(),
    )
    out_specs = (P("ens", "lon", None), P("ens", "lon", None))
    return jax.shard_map(shards, mesh=mesh, in_specs=in_specs, out_specs=out_specs, check_vma=False)
```

```python
import functools

import jax
import jax.numpy as jnp
from jax import lax
from jax.experimental import pallas as pl
from jax.experimental.pallas import tpu as pltpu
from jax.sharding import PartitionSpec as P

BF16 = jnp.bfloat16
F32 = jnp.float32


def dot(a, b):
    return jnp.dot(a, b, preferred_element_type=F32)


def silu_of_twice(h):
    return (h + h * jnp.tanh(h)).astype(BF16)


def nets(half_cols, sun_col, w):
    long_in, long_out, short_in, short_sun, short_mid, short_out = w
    half_sun = sun_col * 0.5
    sun_row = short_sun[...]
    first = silu_of_twice(dot(half_cols, short_in[...]) + half_sun * sun_row)
    hidden = silu_of_twice(dot(half_cols, long_in[...]))
    second = silu_of_twice(dot(first, short_mid[0]) * 0.5)
    third = silu_of_twice(dot(second, short_mid[1]) * 0.5)
    long_tend = dot(hidden, long_out[...])
    short_tend = dot(third, short_out[...])
    return long_tend + jnp.where(sun_col > 0.0, short_tend, 0.0)


def lit_sun_column(day_ref, sun_ref, row0, rows):
    lit = jnp.where(day_ref[...] > 0, sun_ref[...], 0.0)
    lane = lax.broadcasted_iota(jnp.int32, lit.shape, 1)
    return jnp.concatenate(
        [
            jnp.sum(jnp.where(lane == row0 + r, lit, 0.0), axis=1, keepdims=True)
            for r in range(rows)
        ],
        axis=0,
    )


def pack_kernel(
    day_hbm, sun_hbm, short_sun_hbm, state, courant, out_b, out_a, sun_row,
    day, sun, short_sun, west, east, wind, sems,
):
    feats, levels = state.shape[-1], courant.shape[-1]
    end = feats + levels
    cells, lat_rows = day.shape
    copies = [
        pltpu.make_async_copy(src, dst, sems.at[k])
        for k, (src, dst) in enumerate((
            (state.at[:, pl.ds(0, 1), :], west),
            (state.at[:, pl.ds(cells - 1, 1), :], east),
            (courant.at[:, pl.ds(cells - 1, 1), :], wind),
            (day_hbm, day),
            (sun_hbm, sun),
            (short_sun_hbm, short_sun),
        ))
    ]
    for copy in copies:
        copy.start()
    for copy in copies[3:]:
        copy.wait()
    odd = lax.rem(lax.axis_index("lon"), 2) == 1
    lit = jnp.where(day[...] > 0, sun[...], 0.0)

    def choose(to_east, to_west):
        a, b = jnp.where(odd, to_west, to_east), jnp.where(odd, to_east, to_west)
        return a.astype(BF16), b.astype(BF16)

    sun_row[...] = short_sun[...].astype(F32).reshape(sun_row.shape)
    for out, row in zip((out_a, out_b), choose(lit[cells - 1 :], lit[:1])):
        out[:, end:] = jnp.zeros((lat_rows, out.shape[1] - end), BF16)
        out[:16, end : end + lat_rows] = jnp.broadcast_to(row, (16, lat_rows))
    for copy in copies[:3]:
        copy.wait()
    out_a[:, :feats], out_b[:, :feats] = choose(east[:, 0, :], west[:, 0, :])
    out_a[:, feats:end] = wind[:, 0, :].astype(BF16)
    out_b[:, feats:end] = wind[:, 0, :].astype(BF16)


def first_kernel(rows, day, sun, state, *rest):
    *w, tend, prov = rest
    row0 = pl.multiple_of(pl.program_id(0) * rows, rows)
    _, cells, feats = state.shape
    cols = rows * cells
    sun_col = lit_sun_column(day, sun, row0, rows)
    own = state[pl.ds(row0, rows)].reshape(cols, feats)
    phys = nets((own * 0.5).astype(BF16), sun_col, w)
    tend[0] = phys.astype(BF16).reshape(rows, cells, feats)
    prov[pl.ds(row0, rows)] = (own + phys).reshape(rows, cells, feats)


def transport(prov, courant, west_prov, west_cour, east_prov):
    rows, cells, feats = prov.shape
    cols = rows * cells
    levels = courant.shape[-1]
    eastward = courant > 0.0

    def upwind(wind, mask, here, there):
        return jnp.concatenate(
            [wind * jnp.where(mask, here[..., k : k + levels], there[..., k : k + levels]) for k in (0, levels)], axis=-1
        )

    sub = lax.broadcasted_iota(jnp.int32, (rows, 8, feats), 1)
    nxt = pltpu.roll(prov.reshape(cols, feats), cols - 1, 0).reshape(rows, cells, feats)
    tail = jnp.where(sub == 7, east_prov[:, None, :], nxt[:, cells - 8 :])
    nxt = jnp.concatenate([nxt[:, : cells - 8], tail], axis=1)
    flux = upwind(courant, eastward, prov, nxt)
    prev = pltpu.roll(flux.reshape(cols, feats), 1, 0).reshape(rows, cells, feats)
    west_wind = jnp.broadcast_to(west_cour[:, None, :], (rows, 8, levels))
    west_here = jnp.broadcast_to(west_prov[:, None, :], (rows, 8, feats))
    face = upwind(west_wind, west_wind > 0.0, west_here, prov[:, :8])
    head = jnp.where(sub == 0, face, prev[:, :8])
    prev = jnp.concatenate([head, prev[:, 8:]], axis=1)
    return prov - (flux - prev)


def second_kernel(
    rows, day, sun, state, courant, halo_b, halo_a, prov_lo, tend_in,
    long_in, long_out, short_in, short_sun, short_mid, short_out,
    new_state, tend, prov, edges, west_wind,
):
    i = pl.program_id(0)
    tiles = pl.num_programs(0) - 1
    half = tiles * rows
    _, cells, feats = state.shape
    cols = rows * cells
    levels = courant.shape[-1]
    end = feats + levels
    lat_rows = day.shape[1]
    odd = lax.rem(lax.axis_index("lon"), 2) == 1

    def column_nets():
        lo = pl.multiple_of(i * rows, rows)
        hi = pl.multiple_of(half + i * rows, rows)

        def sides(at, n, lanes):
            a, b = halo_a[pl.ds(at, n), lanes].astype(F32), halo_b[pl.ds(at, n), lanes].astype(F32)
            return jnp.where(odd, a, b), jnp.where(odd, b, a)

        west_lo, east_lo = sides(lo, rows, slice(0, feats))
        west_hi, east_hi = sides(hi, rows, slice(0, feats))
        halos = [west_lo, west_hi, east_lo, east_hi]
        west_sun, east_sun = sides(0, 16, slice(end, end + 128))
        lane = lax.broadcasted_iota(jnp.int32, (rows, 128), 1)
        sub = lax.broadcasted_iota(jnp.int32, (rows, 128), 0)
        suns = [
            jnp.sum(jnp.where(lane == sub + at, lit, 0.0), axis=1, keepdims=True)
            for lit, at in ((west_sun, lo), (west_sun, hi), (east_sun, lo), (east_sun, hi))
        ]
        sun_all = jnp.concatenate([lit_sun_column(day, sun, hi, rows)] + suns, axis=0)
        own = state[pl.ds(hi, rows)].reshape(cols, feats)
        half_cols = (jnp.concatenate([own] + halos, axis=0) * 0.5).astype(BF16)
        phys = nets(half_cols, sun_all, (long_in, long_out, short_in, short_sun, short_mid, short_out))
        tend[0] = phys[:cols].astype(BF16).reshape(rows, cells, feats)
        prov[...] = (own + phys[:cols]).reshape(rows, cells, feats)
        edges[...] = jnp.concatenate(halos, axis=0) + phys[cols:]
        west_wind[:rows] = sides(lo, rows, slice(feats, end))[0]
        west_wind[rows:] = sides(hi, rows, slice(feats, end))[0]

    def move():
        lo = pl.multiple_of((i - 1) * rows, rows)
        new_state[0] = transport(
            prov_lo[pl.ds(lo, rows)], courant[pl.ds(lo, rows)],
            edges[:rows], west_wind[:rows], edges[2 * rows : 3 * rows],
        )
        new_state[1] = transport(
            prov[...], courant[pl.ds(half + lo, rows)],
            edges[rows : 2 * rows], west_wind[rows:], edges[3 * rows :],
        )

    @pl.when(i == 0)
    def _():
        column_nets()

    @pl.when(jnp.logical_and(i > 0, i < tiles))
    def _():
        move()
        column_nets()

    @pl.when(i == tiles)
    def _():
        move()


def shards(
    state, courant, daylit, insolation, long_in, long_out, short_in, short_sun, short_mid, short_out
):
    lat_rows, cells, feats = state.shape
    levels = courant.shape[-1]
    hid = long_in.shape[1]
    size = lax.axis_size("lon")
    rows = 16
    half = lat_rows // 2
    steps = half // rows
    width = feats + levels + 128
    day_t, sun_t = daylit.T, insolation.T
    in_vmem = pl.BlockSpec(memory_space=pltpu.VMEM)
    in_hbm = pl.BlockSpec(memory_space=pltpu.HBM)
    edge = pltpu.VMEM((lat_rows, width), BF16)
    edge_b, edge_a, sun_row = pl.pallas_call(
        pack_kernel,
        in_specs=[in_hbm] * 5,
        out_specs=(in_vmem,) * 3,
        out_shape=(edge, edge, pltpu.VMEM((1, hid), F32)),
        scratch_shapes=[
            pltpu.VMEM((cells, lat_rows), jnp.int32),
            pltpu.VMEM((cells, lat_rows), F32),
            pltpu.VMEM((hid,), BF16),
            pltpu.VMEM((lat_rows, 1, feats), F32),
            pltpu.VMEM((lat_rows, 1, feats), F32),
            pltpu.VMEM((lat_rows, 1, levels), F32),
            pltpu.SemaphoreType.DMA((6,)),
        ],
        compiler_params=pltpu.CompilerParams(vmem_limit_bytes=8 * 2**20),
        cost_estimate=pl.CostEstimate(flops=8 * 10**9, bytes_accessed=8 * 2**20, transcendentals=0),
        name="edges_packed",
    )(*(pltpu.with_memory_space_constraint(x, pltpu.HBM) for x in (day_t, sun_t, short_sun, state, courant)))
    flip = [(i, i ^ 1) for i in range(size)]
    seam = [(i, (i + 1 if i % 2 else i - 1) % size) for i in range(size)]
    halo_b = lax.ppermute(edge_b, "lon", seam)
    halo_a = lax.ppermute(edge_a, "lon", flip)

    def vmem(x):
        return pltpu.with_memory_space_constraint(x, pltpu.VMEM)

    weights = (vmem(long_in), vmem(long_out), vmem(short_in), sun_row, vmem(short_mid), vmem(short_out))
    macs = 4 * feats * hid + 2 * hid * hid
    params = pltpu.CompilerParams(vmem_limit_bytes=30 * 2**20)
    tend_shape = pltpu.HBM((2, half, cells, feats), BF16)
    v_state, v_day, v_sun = vmem(state), vmem(day_t), vmem(sun_t)
    tend, prov_lo = pl.pallas_call(
        functools.partial(first_kernel, rows),
        grid=(steps,),
        in_specs=[in_vmem] * 9,
        out_specs=(pl.BlockSpec((1, rows, cells, feats), lambda i: (0, i, 0, 0)), in_vmem),
        out_shape=(tend_shape, pltpu.VMEM((half, cells, feats), F32)),
        compiler_params=params,
        cost_estimate=pl.CostEstimate(
            flops=2 * half * cells * macs, bytes_accessed=2 * 2**20, transcendentals=0
        ),
        name="nets_first_half",
    )(v_day, v_sun, v_state, *weights)

    def here(i):
        return jnp.minimum(i, steps - 1)

    def before(i):
        return jnp.maximum(i - 1, 0)

    new_state, tend = pl.pallas_call(
        functools.partial(second_kernel, rows),
        grid=(steps + 1,),
        in_specs=[in_vmem] * 7 + [in_hbm] + [in_vmem] * 6,
        out_specs=(
            pl.BlockSpec((2, rows, cells, feats), lambda i: (0, before(i), 0, 0)),
            pl.BlockSpec((1, rows, cells, feats), lambda i: (1, here(i), 0, 0)),
        ),
        out_shape=(jax.ShapeDtypeStruct((2, half, cells, feats), F32), tend_shape),
        input_output_aliases={7: 1},
        scratch_shapes=[
            pltpu.VMEM((rows, cells, feats), F32),
            pltpu.VMEM((4 * rows, feats), F32),
            pltpu.VMEM((2 * rows, levels), F32),
        ],
        compiler_params=params,
        cost_estimate=pl.CostEstimate(
            flops=2 * half * (cells + 4) * macs, bytes_accessed=12 * 2**20, transcendentals=0
        ),
        name="nets_second_half_transport",
    )(v_day, v_sun, v_state, vmem(courant), vmem(halo_b), vmem(halo_a), vmem(prov_lo), tend, *weights)
    return new_state.reshape(state.shape), tend.reshape(state.shape)


def solution(mesh):
    in_specs = (
        P("ens", "lon", None),
        P("ens", "lon", None),
        P("ens", "lon"),
        P("ens", "lon"),
        P(),
        P(),
        P(),
        P(),
        P(),
        P(),
    )
    out_specs = (P("ens", "lon", None), P("ens", "lon", None))
    return jax.shard_map(shards, mesh=mesh, in_specs=in_specs, out_specs=out_specs, check_vma=False)
```
